32 devices in a mesh: frame: 4 (over x, core), pixel: 8 (over z, y).
Axes of the slice: x: 2, y: 2, z: 4, core: 2. Of those that a mesh axis runs over, the one named last changes fastest.
Arguments:
- frames: bfloat16 [1024, 16384], P('frame', 'pixel'), may hold values from -6 to 6
- dead_time: float32 [16384], P('pixel'), may hold values from 0.002 to 0.02
- band_width: int32 [16384], P('pixel'), may hold values from 0 to 8
- cycle_label: int32 [16384], P('pixel'), may hold values from 0 to 1, as said below
- valid: int32 [16384], P('pixel'), may hold values from 0 to 1
Outputs:
- two_time: float32 [1024, 2, 1024], P(('frame', 'pixel'))
The draws below stay inside these ranges and needn't reach their ends.
Inputs may be any that keep to these rules, and one draw needn't show every extreme that they name: `cycle_label`: every cycle holds at least one pixel with valid 1.
All inputs are finite; a program needn't handle non-finite values.
Results may differ from the reference program's by a relative error of at most 0.004.
Values may be sent and summed in bfloat16 or wider, within the bound.
No kernel may reach another device: no remote copies, remote signals or barrier semaphores. Data moves between devices by JAX's collectives and lax.ppermute only.
A program may use at most 64 MiB of HBM per device.

```python
import math
import jax
import jax.numpy as jnp
from jax import lax

NFRAMES = 1024
CYCLES = 2
BAND = 8
NPIX = 16384


def draw_cycle_label(key, part):
    first = jax.random.randint(jax.random.fold_in(key, 11), (NPIX,), 0, CYCLES)
    second = jax.random.randint(jax.random.fold_in(key, 12), (NPIX,), 0, CYCLES)
    labels = jnp.minimum(first, second)
    position = jnp.arange(NPIX, dtype=jnp.int32)
    return jnp.where(position < CYCLES, position, labels).astype(jnp.int32)


def draw_valid(key, part):
    drawn = jax.random.randint(jax.random.fold_in(key, 21), (NPIX,), 0, 8)
    position = jnp.arange(NPIX, dtype=jnp.int32)
    return jnp.where((drawn < 7) | (position < CYCLES), 1, 0).astype(jnp.int32)


def set_ends(entries, stream_key, low, high):
    extent = entries.shape
    index_at = [jax.random.randint(jax.random.fold_in(stream_key, axis), (), 0, extent[axis]) for axis in range(len(extent))]
    entries = entries.at[tuple(index_at)].set(low)
    longest = extent.index(max(extent))
    index_at[longest] = (index_at[longest] + 1) % extent[longest]
    return entries.at[tuple(index_at)].set(high)


def with_spikes(values, stream_key, source, target, blocks, factor):
    owner, partner = [(jnp.arange(values.shape[axis_at]) // (values.shape[axis_at] // blocks)).reshape([-1 if axis == axis_at else 1 for axis in range(values.ndim)]) for axis_at in (source, target)]
    chosen = jax.random.permutation(stream_key, blocks)[partner]
    strong = (owner == chosen) | (owner == (partner + blocks // 2) % blocks)
    return jnp.where(strong, factor * values, values)


def level_of(key, shape, split, smallest, top_value):
    def one(dim, blocks):
        heights = jax.random.uniform(jax.random.fold_in(jax.random.fold_in(key, 6), dim), (blocks,), jnp.float32, smallest / len(split), top_value / len(split))
        return jnp.repeat(jnp.exp(heights), shape[dim] // blocks).reshape((-1,) + (1,) * (len(shape) - dim - 1))

    level = one(*split[0])
    for cut in split[1:]:
        level = level * one(*cut)
    return level


def noise_with(key, shape, scale, most, split, heavy, held_as=jnp.bfloat16):
    result = scale * jax.random.normal(key, shape, jnp.float32)
    if split:
        result = result * level_of(key, shape, split, -0.22, 0.18)
    return jnp.clip(with_spikes(result, jax.random.fold_in(key, 3), *heavy), -most, most).astype(held_as)


def setup_inputs(seed: int = 0) -> dict:
    splits = jax.random.split(jax.random.key(seed), 6)
    return {
        "frames": noise_with(splits[0], (NFRAMES, NPIX), 1.0, 6.0, ((0, 4), (1, 8)), (1, 0, 8, 2.0)),
        "dead_time": jnp.clip(jnp.exp(math.log(0.02) - 2.30258502 * jax.random.uniform(splits[1], (NPIX,), jnp.float32) ** level_of(splits[1], (NPIX,), ((0, 8),), -0.2, 0.2)), 0.002, 0.02),
        "band_width": set_ends(jax.random.randint(splits[2], (NPIX,), 0, BAND + 1), jax.random.fold_in(splits[2], 1), 0, BAND).astype(jnp.int32),
        "cycle_label": draw_cycle_label(jax.random.fold_in(splits[5], 71), 0),
        "valid": draw_valid(jax.random.fold_in(splits[5], 71), 0),
    }


def smooth_block(frame_block, dead_block, width_block):
    count_rate = 4.0 + frame_block.astype(jnp.float32)
    corrected = count_rate / (1.0 - dead_block[None, :] * count_rate)
    running = jnp.concatenate([jnp.zeros((1, corrected.shape[1]), jnp.float32), jnp.cumsum(corrected, axis=0)], axis=0)
    frame_idx = jnp.arange(NFRAMES, dtype=jnp.int32)[:, None]
    upper_end = jnp.minimum(frame_idx + width_block[None, :], NFRAMES - 1)
    lower_end = jnp.maximum(frame_idx - width_block[None, :], 0)
    total = jnp.take_along_axis(running, upper_end + 1, axis=0) - jnp.take_along_axis(running, lower_end, axis=0)
    return (total / (upper_end - lower_end + 1).astype(jnp.float32)).astype(jnp.bfloat16)


def reference(frames, dead_time, band_width, cycle_label, valid):
    npix_all = frames.shape[1]
    block = math.gcd(npix_all, 4096)
    nblocks = npix_all // block
    cycle_ids = jnp.arange(CYCLES, dtype=jnp.int32)[:, None]

    def step(index, carry):
        gram, cycle_sum, counts = carry
        begin = (index * block).astype(jnp.int32)
        frame_block = lax.dynamic_slice_in_dim(frames, begin, block, 1)
        dead_block = lax.dynamic_slice_in_dim(dead_time, begin, block, 0)
        width_block = lax.dynamic_slice_in_dim(band_width, begin, block, 0)
        label_block = lax.dynamic_slice_in_dim(cycle_label, begin, block, 0)
        valid_block = lax.dynamic_slice_in_dim(valid, begin, block, 0)
        smoothed = smooth_block(frame_block, dead_block, width_block)
        member = ((label_block[None, :] == cycle_ids) & (valid_block[None, :] == 1)).astype(jnp.bfloat16)
        counts = counts + jnp.sum(member.astype(jnp.float32), axis=1)
        cycle_sum = cycle_sum + lax.dot_general(smoothed, member, (((1,), (1,)), ((), ())), preferred_element_type=jnp.float32)
        weighted = (smoothed[:, None, :] * member[None, :, :]).reshape(NFRAMES * CYCLES, block)
        product = lax.dot_general(weighted, smoothed, (((1,), (1,)), ((), ())), preferred_element_type=jnp.float32)
        gram = gram + product.reshape(NFRAMES, CYCLES, NFRAMES)
        return gram, cycle_sum, counts

    start = (jnp.zeros((NFRAMES, CYCLES, NFRAMES), jnp.float32), jnp.zeros((NFRAMES, CYCLES), jnp.float32), jnp.zeros((CYCLES,), jnp.float32))
    gram, cycle_sum, counts = lax.fori_loop(0, nblocks, step, start)
    mean = cycle_sum / counts[None, :]
    return gram / counts[None, :, None] - mean[:, :, None] * jnp.transpose(mean)[None, :, :]
```

```python
import functools
import jax
import jax.numpy as jnp
from jax import lax
from jax.experimental import pallas as pl
from jax.experimental.pallas import tpu as pltpu
from jax.sharding import PartitionSpec as P

CYCLES = 2
BAND = 8
HALO = 16
LANE = 128
f32 = jnp.float32
bf16 = jnp.bfloat16
NT = (((1,), (1,)), ((), ()))


def cost(flops, nbytes):
    return pl.CostEstimate(flops=flops, bytes_accessed=nbytes, transcendentals=0)


def correct(raw, dead):
    rate = 4.0 + raw.astype(f32)
    return rate / (1.0 - dead * rate)


def band_sum(c_ref, at, n, lanes, width):
    acc = c_ref[pl.ds(at, n), lanes]
    for k in range(1, BAND + 1):
        pair = c_ref[pl.ds(at - k, n), lanes] + c_ref[pl.ds(at + k, n), lanes]
        acc = acc + jnp.where(width >= k, pair, 0.0)
    return acc


def middle_kernel(raw_ref, dead_ref, width_ref, out_ref, c_ref, *, tile):
    rows, px = raw_ref.shape
    quarter = rows // 4
    for col in range(px // LANE):
        lanes = pl.ds(col * LANE, LANE)
        dead = dead_ref[lanes][None, :]
        width = width_ref[lanes][None, :]
        inverse = 1.0 / (2 * width + 1).astype(f32)
        c_ref[:, lanes] = correct(raw_ref[pl.ds(quarter - HALO, 2 * quarter + 2 * HALO), lanes], dead)
        for r in range(2 * quarter // tile):
            acc = band_sum(c_ref, HALO + r * tile, tile, lanes, width)
            out_ref[pl.ds(r * tile, tile), lanes] = (acc * inverse).astype(bf16)


def edge_kernel(raw_ref, up_ref, down_ref, dead_ref, width_ref, out_ref, c_ref, *, tile, nframes):
    rows, px = raw_ref.shape
    quarter = rows // 4
    block = lax.axis_index("frame")
    begin = block * rows
    has_up = (block > 0).astype(f32)
    has_down = ((block + 1) * rows < nframes).astype(f32)
    span = quarter + 2 * HALO
    for col in range(px // LANE):
        lanes = pl.ds(col * LANE, LANE)
        dead = dead_ref[lanes][None, :]
        width = width_ref[lanes][None, :]
        c_ref[pl.ds(0, HALO), lanes] = correct(up_ref[:, lanes], dead) * has_up
        c_ref[pl.ds(HALO, quarter + HALO), lanes] = correct(raw_ref[pl.ds(0, quarter + HALO), lanes], dead)
        c_ref[pl.ds(span, quarter + HALO), lanes] = correct(raw_ref[pl.ds(rows - quarter - HALO, quarter + HALO), lanes], dead)
        c_ref[pl.ds(span + quarter + HALO, HALO), lanes] = correct(down_ref[:, lanes], dead) * has_down
        for half in range(2):
            for r in range(quarter // tile):
                acc = band_sum(c_ref, half * span + HALO + r * tile, tile, lanes, width)
                first = begin + half * (rows - quarter) + r * tile
                t = first + lax.broadcasted_iota(jnp.int32, (tile, LANE), 0)
                terms = jnp.minimum(t + width, nframes - 1) - jnp.maximum(t - width, 0) + 1
                out_ref[pl.ds(half * quarter + r * tile, tile), lanes] = (acc / terms.astype(f32)).astype(bf16)


def smooth_middle(raw, dead, width):
    rows, px = raw.shape
    lanes = min(px, 1024)
    return pl.pallas_call(
        functools.partial(middle_kernel, tile=min(32, rows // 4)),
        grid=(px // lanes,),
        in_specs=[pl.BlockSpec((rows, lanes), lambda i: (0, i))] + [pl.BlockSpec((lanes,), lambda i: (i,))] * 2,
        out_specs=pl.BlockSpec((rows // 2, lanes), lambda i: (0, i)),
        out_shape=jax.ShapeDtypeStruct((rows // 2, px), bf16),
        scratch_shapes=[pltpu.VMEM((rows // 2 + 2 * HALO, lanes), f32)],
        cost_estimate=cost(rows * px * 60, rows * px * 3),
        name="smooth_middle",
    )(raw, dead, width)


def smooth_edges(raw, up, down, dead, width, nframes):
    rows, px = raw.shape
    lanes = min(px, 1024)
    column = lambda i: (0, i)
    return pl.pallas_call(
        functools.partial(edge_kernel, tile=min(32, rows // 4), nframes=nframes),
        grid=(px // lanes,),
        in_specs=[pl.BlockSpec((rows, lanes), column)]
        + [pl.BlockSpec((HALO, lanes), column)] * 2
        + [pl.BlockSpec((lanes,), lambda i: (i,))] * 2,
        out_specs=pl.BlockSpec((rows // 2, lanes), column),
        out_shape=jax.ShapeDtypeStruct((rows // 2, px), bf16),
        scratch_shapes=[pltpu.VMEM((rows // 2 + 4 * HALO, lanes), f32)],
        cost_estimate=cost(rows * px * 60, rows * px * 3),
        name="smooth_edges",
    )(raw, up, down, dead, width)


def gram_kernel(label_ref, valid_ref, mid_ref, edge_ref, *refs, ncols, own):
    cols, rest = refs[:ncols], refs[ncols:]
    out_ref, acc_ref = rest[0], rest[-1]
    half, px = mid_ref.shape
    quarter = half // 2
    rows = 2 * half
    step = pl.program_id(0)
    label = label_ref[...][None, :]
    used = valid_ref[...][None, :] == 1
    member = [((label == q) & used).astype(f32) for q in range(CYCLES)]
    weight = [jnp.broadcast_to(m, (16, px)).astype(bf16) for m in member]
    mid, edge = mid_ref[...], edge_ref[...]
    natural = jnp.concatenate([edge[:quarter], mid, edge[quarter:]], axis=0)
    left = jnp.concatenate([natural * w[:1] for w in weight] + weight, axis=0)
    right = jnp.concatenate([c[...] for c in cols] + [jnp.ones((LANE, px), bf16)], axis=0)
    product = lax.dot_general(left, right, NT, preferred_element_type=f32)

    @pl.when(step == 0)
    def _():
        acc_ref[...] = product

    @pl.when(step > 0)
    def _():
        acc_ref[...] += product

    @pl.when(step == pl.num_programs(0) - 1)
    def _():
        width = out_ref.shape[-1]
        for q in range(CYCLES):
            base = CYCLES * rows + 16 * q
            count = acc_ref[pl.ds(base, 1), pl.ds(width, LANE)]
            mean = acc_ref[pl.ds(base, 1), pl.ds(0, width)] / jnp.maximum(count[:, :1], 1.0)
            total = acc_ref[pl.ds(q * rows, rows), pl.ds(width, LANE)]
            for j in range(width // LANE):
                lanes = pl.ds(j * LANE, LANE)
                block = acc_ref[pl.ds(q * rows, rows), lanes]
                out_ref[q, :, lanes] = (block - total * mean[:, j * LANE : (j + 1) * LANE]).astype(bf16)
            if own:
                rest[1][pl.ds(q, 1), :] = mean[:, :rows]
                rest[1][pl.ds(CYCLES + q, 1), :] = jnp.broadcast_to(count[:, :1], (1, rows))


def gram(label, valid, mid, edge, cols, own):
    half, px = mid.shape
    rows = 2 * half
    lanes = min(px, 1024)
    width = sum(c.shape[0] for c in cols)
    column = lambda i: (0, i)
    whole = lambda *shape: pl.BlockSpec(shape, lambda i: (0,) * len(shape))
    out_shape = [jax.ShapeDtypeStruct((CYCLES, rows, width), bf16)]
    out_specs = [whole(CYCLES, rows, width)]
    if own:
        out_shape.append(jax.ShapeDtypeStruct((2 * CYCLES, rows), f32))
        out_specs.append(whole(2 * CYCLES, rows))
    return pl.pallas_call(
        functools.partial(gram_kernel, ncols=len(cols), own=own),
        grid=(px // lanes,),
        in_specs=[pl.BlockSpec((lanes,), lambda i: (i,))] * 2
        + [pl.BlockSpec((s.shape[0], lanes), column) for s in (mid, edge, *cols)],
        out_specs=out_specs,
        out_shape=out_shape,
        scratch_shapes=[pltpu.VMEM((CYCLES * (rows + 16), width + LANE), f32)],
        cost_estimate=cost(2 * CYCLES * rows * width * px, 2 * (rows + width) * px),
        name="gram_own" if own else "gram_cross",
    )(label, valid, mid, edge, *cols)


def shards(frames, dead_time, band_width, cycle_label, valid):
    nblocks = lax.axis_size("frame")
    ngroups = lax.axis_size("pixel")
    rows = frames.shape[0]
    nframes = rows * nblocks
    half, quarter = rows // 2, rows // 4
    own_rows = rows // ngroups
    me, group = lax.axis_index("frame"), lax.axis_index("pixel")

    def swap(x, axis, bit):
        return lax.ppermute(x, axis, [(i, i ^ bit) for i in range(lax.axis_size(axis))])

    down = lax.ppermute(frames[:HALO], "frame", [(i + 1, i) for i in range(nblocks - 1)])
    up = lax.ppermute(frames[rows - HALO :], "frame", [(i, i + 1) for i in range(nblocks - 1)])
    mid = smooth_middle(frames, dead_time, band_width)
    far_mid = {j: swap(mid, "frame", j) for j in range(2, nblocks, 2)}
    near_mid = swap(mid, "frame", 1)
    edge = smooth_edges(frames, up, down, dead_time, band_width, nframes)
    far_edge = {j: swap(edge, "frame", j) for j in range(2, nblocks, 2)}
    near_edge = swap(edge, "frame", 1)

    def reduce(x, stats):
        x = x.reshape(CYCLES, ngroups, own_rows, x.shape[-1])
        bit = 1
        while bit < ngroups:
            x = x.reshape(CYCLES, -1, 2, own_rows, x.shape[-1])
            mine = (group // bit) % 2
            keep = lax.dynamic_index_in_dim(x, mine, 2, keepdims=False)
            send = lax.dynamic_index_in_dim(x, 1 - mine, 2, keepdims=False)
            x = keep.astype(f32) + swap(send, "pixel", bit).astype(f32)
            if stats is not None:
                stats = jnp.concatenate([stats, swap(stats, "pixel", bit)], axis=0)
            bit *= 2
            if bit < ngroups:
                x = x.astype(bf16)
        return x.reshape(CYCLES, own_rows, x.shape[-1]), stats

    own, stats = gram(cycle_label, valid, mid, edge, (mid, edge, near_mid, near_edge), True)
    own, stats = reduce(own, stats[None])
    mids = [own[..., :half], own[..., rows : rows + half]]
    edges = [own[..., half:rows], own[..., rows + half :]]
    all_stats = [stats, swap(stats, "frame", 1)]
    for j in range(2, nblocks, 2):
        far = swap(stats, "frame", j)
        all_stats += [far, swap(far, "frame", 1)]
        for source, parts in ((far_mid[j], mids), (far_edge[j], edges)):
            part = gram(cycle_label, valid, mid, edge, (source, swap(source, "frame", 1)), False)[0]
            part = reduce(part, None)[0]
            parts += [part[..., :half], part[..., half:]]

    def natural(m, e):
        return jnp.concatenate([e[..., :quarter], m, e[..., quarter:]], axis=-1)

    def in_order(blocks):
        bit = 1
        while bit < nblocks:
            swapped = [blocks[j ^ bit] for j in range(nblocks)]
            flip = (me // bit) % 2 == 1
            blocks = [jnp.where(flip, s, b) for s, b in zip(swapped, blocks)]
            bit *= 2
        return jnp.concatenate(blocks, axis=-1)

    all_stats = [natural(s[..., :half], s[..., half:]) for s in all_stats]
    row_stats = lax.dynamic_slice_in_dim(all_stats[0], group * own_rows, own_rows, 2)
    all_stats = in_order(all_stats)
    number = all_stats[:, CYCLES:, :1]
    counts = jnp.sum(number, axis=0)
    share = number / counts
    grand = jnp.sum(all_stats[:, :CYCLES] * share, axis=0)
    grand_rows = jnp.sum(row_stats[:, :CYCLES] * share, axis=0)
    between = jnp.einsum(
        "dqr,dqc->qrc",
        (row_stats[:, :CYCLES] - grand_rows) * share,
        all_stats[:, :CYCLES] - grand,
        precision=lax.Precision.HIGHEST,
    )
    within = in_order([natural(m, e) for m, e in zip(mids, edges)])
    return jnp.transpose(within / counts[:, :, None] + between, (1, 0, 2))


def solution(mesh):
    in_specs = (P("frame", "pixel"), P("pixel"), P("pixel"), P("pixel"), P("pixel"))
    out_specs = P(("frame", "pixel"), None, None)
    return jax.shard_map(shards, mesh=mesh, in_specs=in_specs, out_specs=out_specs, check_vma=False)
```

```python
import functools
import jax
import jax.numpy as jnp
from jax import lax
from jax.experimental import pallas as pl
from jax.experimental.pallas import tpu as pltpu
from jax.sharding import PartitionSpec as P

CYCLES = 2
BAND = 8
HALO = 16
EDGE_PART = 4
STAT = 8
STAT_ROWS = 16
LANE = 128
f32 = jnp.float32
bf16 = jnp.bfloat16
NT = (((1,), (1,)), ((), ()))
NN = (((1,), (0,)), ((), ()))
EXACT = lax.Precision.HIGHEST


def kernel_call(body, name, args, outs, scratch=(), in_specs=None, mib=4):
    vmem = pl.BlockSpec(memory_space=pltpu.VMEM)
    return pl.pallas_call(
        body,
        in_specs=in_specs or [vmem] * len(args),
        out_specs=[vmem] * len(outs),
        out_shape=[jax.ShapeDtypeStruct(shape, dtype) for shape, dtype in outs],
        scratch_shapes=list(scratch),
        compiler_params=pltpu.CompilerParams(vmem_limit_bytes=mib * 2**20),
        cost_estimate=pl.CostEstimate(flops=0, bytes_accessed=2**18, transcendentals=0),
        name=name,
    )(*args)


def correct(raw, dead):
    rate = 4.0 + raw.astype(f32)
    return rate / (1.0 - dead * rate)


def band_sum(c_ref, at, n, width):
    acc = c_ref[pl.ds(at, n), :]
    for k in range(1, BAND + 1):
        pair = c_ref[pl.ds(at - k, n), :] + c_ref[pl.ds(at + k, n), :]
        acc = acc + jnp.where(width >= k, pair, 0.0)
    return acc


def halo_kernel(frames_ref, near_ref, far_ref, ends_ref, sems):
    rows = frames_ref.shape[0]
    copies = [
        pltpu.make_async_copy(frames_ref.at[pl.ds(at, HALO)], ends_ref.at[i], sems.at[i])
        for i, at in enumerate((0, rows - HALO))
    ]
    for copy in copies:
        copy.start()
    for copy in copies:
        copy.wait()
    even = lax.axis_index("frame") % 2 == 0
    first, last = ends_ref[0], ends_ref[1]
    far_ref[...] = jnp.where(even, first, last)
    near_ref[...] = jnp.where(even, last, first)


def halos(frames):
    rows, px = frames.shape
    return kernel_call(
        halo_kernel,
        "halos",
        (frames,),
        [((HALO, px), bf16)] * 2,
        [pltpu.VMEM((2, HALO, px), bf16), pltpu.SemaphoreType.DMA((2,))],
        in_specs=[pl.BlockSpec(memory_space=pltpu.HBM)],
    )


def middle_kernel(frames_ref, dead_hbm, width_hbm, mid_ref, rim_ref, dead_ref, width_ref, raw_ref, c_ref, sems):
    rows, px = frames_ref.shape
    edge = rim_ref.shape[0] // 2 - HALO
    tile = 32
    chunk = min(512, px)
    small = [pltpu.make_async_copy(dead_hbm, dead_ref, sems.at[0]), pltpu.make_async_copy(width_hbm, width_ref, sems.at[1])]
    large = [
        pltpu.make_async_copy(frames_ref.at[:, pl.ds(i * chunk, chunk)], raw_ref.at[:, pl.ds(i * chunk, chunk)], sems.at[2 + i])
        for i in range(px // chunk)
    ]
    for copy in small + large:
        copy.start()
    for copy in small:
        copy.wait()
    for i, copy in enumerate(large):
        copy.wait()
        part = pl.ds(i * chunk, chunk)
        rim_ref[pl.ds(0, edge + HALO), part] = raw_ref[pl.ds(0, edge + HALO), part]
        rim_ref[pl.ds(edge + HALO, edge + HALO), part] = raw_ref[pl.ds(rows - edge - HALO, edge + HALO), part]
        for col in range(chunk // LANE):
            lanes = pl.ds(i * chunk + col * LANE, LANE)
            dead = dead_ref[lanes][None, :]
            width = width_ref[lanes][None, :]
            inverse = 1.0 / (2 * width + 1).astype(f32)
            c_ref[...] = correct(raw_ref[pl.ds(edge - HALO, rows - 2 * edge + 2 * HALO), lanes], dead)
            for r in range((rows - 2 * edge) // tile):
                acc = band_sum(c_ref, HALO + r * tile, tile, width)
                mid_ref[pl.ds(r * tile, tile), lanes] = (acc * inverse).astype(bf16)


def edge_kernel(rim_ref, near_ref, far_ref, dead_ref, width_ref, out_ref, c_ref, *, nframes):
    px = rim_ref.shape[1]
    edge = out_ref.shape[0] // 2
    rows = nframes // lax.axis_size("frame")
    tile = 32
    block = lax.axis_index("frame")
    even = block % 2 == 0
    begin = block * rows
    has_up = (block > 0).astype(f32)
    has_down = ((block + 1) * rows < nframes).astype(f32)
    span = edge + 2 * HALO
    for col in range(px // LANE):
        lanes = pl.ds(col * LANE, LANE)
        dead = dead_ref[lanes][None, :]
        width = width_ref[lanes][None, :]
        near, far = near_ref[:, lanes], far_ref[:, lanes]
        c_ref[pl.ds(0, HALO), :] = correct(jnp.where(even, far, near), dead) * has_up
        c_ref[pl.ds(HALO, edge + HALO), :] = correct(rim_ref[pl.ds(0, edge + HALO), lanes], dead)
        c_ref[pl.ds(span, edge + HALO), :] = correct(rim_ref[pl.ds(edge + HALO, edge + HALO), lanes], dead)
        c_ref[pl.ds(span + edge + HALO, HALO), :] = correct(jnp.where(even, near, far), dead) * has_down
        for half in range(2):
            for r in range(edge // tile):
                acc = band_sum(c_ref, half * span + HALO + r * tile, tile, width)
                first = begin + half * (rows - edge) + r * tile
                t = first + lax.broadcasted_iota(jnp.int32, (tile, LANE), 0)
                terms = jnp.minimum(t + width, nframes - 1) - jnp.maximum(t - width, 0) + 1
                out_ref[pl.ds(half * edge + r * tile, tile), lanes] = (acc / terms.astype(f32)).astype(bf16)


def smooth_middle(frames, dead, width, edge):
    rows, px = frames.shape
    mid = rows - 2 * edge
    return kernel_call(
        middle_kernel,
        "smooth_middle",
        (frames, dead, width),
        [((mid, px), bf16), ((2 * (edge + HALO), px), bf16), ((px,), f32), ((px,), jnp.int32)],
        [pltpu.VMEM((rows, px), bf16), pltpu.VMEM((mid + 2 * HALO, LANE), f32), pltpu.SemaphoreType.DMA((2 + px // min(512, px),))],
        in_specs=[pl.BlockSpec(memory_space=pltpu.HBM)] * 3,
    )


def smooth_edges(rim, near, far, dead, width, nframes):
    edge = rim.shape[0] // 2 - HALO
    return kernel_call(
        functools.partial(edge_kernel, nframes=nframes),
        "smooth_edges",
        (rim, near, far, dead, width),
        [((2 * edge, rim.shape[1]), bf16)],
        [pltpu.VMEM((2 * (edge + 2 * HALO), LANE), f32)],
    )[0]


def hold_kernel(*refs):
    pass


def hold(x, *tokens):
    anywhere = pl.BlockSpec(memory_space=pl.ANY)
    return pl.pallas_call(
        hold_kernel,
        in_specs=[anywhere] * (1 + len(tokens)),
        out_specs=anywhere,
        out_shape=jax.ShapeDtypeStruct(x.shape, x.dtype),
        input_output_aliases={0: 0},
        compiler_params=pltpu.CompilerParams(vmem_limit_bytes=2**20),
        cost_estimate=pl.CostEstimate(flops=0, bytes_accessed=0, transcendentals=0),
        name="hold",
    )(x, *tokens)


def tree_order(n):
    return [0] if n == 1 else [2 * s + bit for bit in range(2) for s in tree_order(n // 2)]


def centre(product_ref, total_ref, mean, keep_ref, send_ref, groups):
    rows = product_ref.shape[0] // CYCLES - 16
    size = rows // groups
    me = lax.axis_index("pixel")
    for at, slot in enumerate(tree_order(groups)):
        out_ref = send_ref if slot % 2 else keep_ref
        place = (at % (groups // 2)) * CYCLES * size
        for q in range(CYCLES):
            begin = pl.multiple_of(q * rows + (me ^ slot) * size, size)
            total = total_ref[pl.ds(begin, size), :]
            for j in range(keep_ref.shape[1] // LANE):
                lanes = pl.ds(j * LANE, LANE)
                centred = product_ref[pl.ds(begin, size), lanes] - total * mean[q][:, j * LANE : (j + 1) * LANE]
                out_ref[pl.ds(place + q * size, size), lanes] = centred.astype(bf16)


def means(product_ref, total_ref, width):
    base = product_ref.shape[0] - 16 * CYCLES
    count = [total_ref[pl.ds(base + 16 * q, 1), :][:, :1] for q in range(CYCLES)]
    mean = [product_ref[pl.ds(base + 16 * q, 1), pl.ds(0, width)] / jnp.maximum(count[q], 1.0) for q in range(CYCLES)]
    return mean, count


def split(x, pieces):
    out = []
    for _ in range(pieces):
        out.append(x.astype(bf16).astype(f32))
        x = x - out[-1]
    return out


def stat_rows(mean, count=None):
    width = mean[0].shape[1]
    rows = [piece for m in zip(*[split(m, 3) for m in mean]) for piece in m]
    zero = jnp.zeros((1, width), f32)
    if count is None:
        rows += [zero] * 2
    else:
        lane = lax.broadcasted_iota(jnp.int32, (1, width), 1) // (LANE // 2)
        for part in zip(*[split(c, 2) for c in count]):
            rows.append(sum(jnp.where(lane == q, p, 0.0) for q, p in enumerate(part)))
    return jnp.concatenate(rows + [zero] * (STAT_ROWS - len(rows)), axis=0).astype(bf16)


def gram_own_kernel(label_ref, valid_ref, mid_ref, edge_ref, *refs, groups):
    near_refs, (out_ref, left_ref, total_ref, acc_ref) = refs[:-4], refs[-4:]
    px = mid_ref.shape[1]
    rim = edge_ref.shape[0] // 2
    rows = mid_ref.shape[0] + 2 * rim
    width = 2 * rows
    label = label_ref[...][None, :]
    used = valid_ref[...][None, :] == 1
    for q in range(CYCLES):
        weight = jnp.broadcast_to(((label == q) & used).astype(f32), (16, px)).astype(bf16)
        left_ref[pl.ds(q * rows, rim), :] = edge_ref[pl.ds(0, rim), :] * weight[:1]
        left_ref[pl.ds(q * rows + rim, rows - 2 * rim), :] = mid_ref[...] * weight[:1]
        left_ref[pl.ds((q + 1) * rows - rim, rim), :] = edge_ref[pl.ds(rim, rim), :] * weight[:1]
        left_ref[pl.ds(CYCLES * rows + 16 * q, 16), :] = weight
    right = jnp.concatenate([ref[...] for ref in (mid_ref, edge_ref, *near_refs)] + [jnp.ones((LANE, px), bf16)], axis=0)
    acc_ref[...] = lax.dot_general(left_ref[...], right, NT, preferred_element_type=f32)
    total_ref[...] = acc_ref[:, pl.ds(width, LANE)]
    mean, count = means(acc_ref, total_ref, width)
    size = rows // groups
    stats = stat_rows(mean, count)
    for group in range(groups):
        for q in range(CYCLES):
            here = pl.ds(q * rows + group * size, size)
            for j in range(width // LANE):
                lanes = pl.ds(j * LANE, LANE)
                centred = acc_ref[here, lanes] - total_ref[here, :] * mean[q][:, j * LANE : (j + 1) * LANE]
                out_ref[group, pl.ds(q * size, size), lanes] = centred.astype(bf16)
        out_ref[group, pl.ds(CYCLES * size, STAT_ROWS), :] = stats


def part_outs(rows, width, stat_rows):
    return [((rows, width), bf16), ((rows + stat_rows, width), bf16), ((stat_rows, width), bf16)]


def gram_own(label, valid, mid, edge, near, groups):
    px = mid.shape[1]
    rows = mid.shape[0] + edge.shape[0]
    tall = CYCLES * (rows + 16)
    return kernel_call(
        functools.partial(gram_own_kernel, groups=groups),
        "gram_own",
        (label, valid, mid, edge, *near),
        [((groups, CYCLES * rows // groups + STAT_ROWS, 2 * rows), bf16), ((tall, px), bf16), ((tall, LANE), f32)],
        [pltpu.VMEM((tall, 2 * rows + LANE), f32)],
        mib=10,
    )


def gram_cross_kernel(left_ref, total_ref, *refs, groups):
    col_refs, (keep_ref, send_ref, stat_ref, acc_ref) = refs[:-4], refs[-4:]
    right = jnp.concatenate([ref[...] for ref in col_refs], axis=0)
    acc_ref[...] = lax.dot_general(left_ref[...], right, NT, preferred_element_type=f32)
    mean, _ = means(acc_ref, total_ref, acc_ref.shape[1])
    stats = stat_rows(mean)
    stat_ref[...] = stats
    send_ref[pl.ds(send_ref.shape[0] - STAT_ROWS, STAT_ROWS), :] = stats
    centre(acc_ref, total_ref, mean, keep_ref, send_ref, groups)


def gram_cross(left, total, cols, groups):
    tall, width = left.shape[0], sum(c.shape[0] for c in cols)
    return kernel_call(
        functools.partial(gram_cross_kernel, groups=groups),
        "gram_cross",
        (left, total, *cols),
        part_outs(tall // 2 - 16, width, STAT_ROWS),
        [pltpu.VMEM((tall, width), f32)],
        mib=8,
    )


def join_stats(mine_ref, got_ref, groups):
    mine = mine_ref[...].astype(f32)
    got = got_ref[pl.ds(got_ref.shape[0] - mine.shape[0], mine.shape[0]), :].astype(f32)
    return jnp.concatenate([mine[: groups * STAT], got[: groups * STAT]], axis=0)


def merge_kernel(keep_ref, got_ref, stat_ref, next_keep_ref, next_send_ref, next_stat_ref, *, groups):
    half = next_keep_ref.shape[0]
    total = keep_ref[...].astype(f32) + got_ref[pl.ds(0, 2 * half), :].astype(f32)
    next_keep_ref[...] = total[:half].astype(bf16)
    next_send_ref[pl.ds(0, half), :] = total[half:].astype(bf16)
    stats = join_stats(stat_ref, got_ref, groups).astype(bf16)
    next_stat_ref[...] = stats
    next_send_ref[pl.ds(half, stats.shape[0]), :] = stats


def merge(keep, got, stat, groups):
    outs = part_outs(keep.shape[0] // 2, keep.shape[1], 2 * groups * STAT)
    return kernel_call(functools.partial(merge_kernel, groups=groups), "merge", (keep, got, stat), outs)


def whole_means(stats):
    n = stats.shape[0]
    return stats + pltpu.roll(stats, n - CYCLES, 0) + pltpu.roll(stats, n - 2 * CYCLES, 0)


def own_part_kernel(got_ref, out_ref, side_ref, share_ref, *, edge):
    groups, _, width = got_ref.shape
    size = out_ref.shape[0] // CYCLES
    rows = width // 2
    mid = rows - 2 * edge
    me = lax.axis_index("pixel")
    stats = [got_ref[me ^ i, pl.ds(CYCLES * size, STAT_ROWS), :].astype(f32)[:STAT] for i in range(groups)]
    stats = jnp.concatenate(stats, axis=0)
    entries = stats.shape[0]
    kind = lax.broadcasted_iota(jnp.int32, (entries, 1), 0) % STAT
    n = me * size + lax.broadcasted_iota(jnp.int32, (size, rows), 0)
    packed = jnp.where(n < edge, n + mid, jnp.where(n < edge + mid, n - edge, n))
    pick = (packed == lax.broadcasted_iota(jnp.int32, (size, rows), 1)).astype(f32)
    counted = stats + pltpu.roll(stats, entries - 1, 0)
    mean = whole_means(stats)
    for q in range(CYCLES):
        number = pltpu.roll(counted, entries - 3 * CYCLES + q, 0)[:, q * LANE // 2 : q * LANE // 2 + 1]
        number = jnp.where(kind == q, number, 0.0)
        count = jnp.sum(number, axis=0, keepdims=True)
        share = number / count
        share_ref[pl.ds(q * entries, entries), :] = jnp.broadcast_to(share, (entries, LANE))
        share_ref[pl.ds(CYCLES * entries + 8 * q, 8), :] = jnp.broadcast_to(1.0 / count, (8, LANE))
        apart = mean[:, :rows] - jnp.sum(mean[:, :rows] * share, axis=0, keepdims=True)
        side = lax.dot_general(pick, apart * share, NT, precision=EXACT, preferred_element_type=f32)
        here = pl.ds(q * size, size)
        side_ref[here, :] = side
        within = got_ref[0, here, :].astype(f32)
        for group in range(1, groups):
            within += got_ref[group, here, :].astype(f32)
        out_ref[here, :] = within * (1.0 / count) + part_between(mean, side, share)


def part_between(mean, side, share):
    apart = mean - jnp.sum(mean * share, axis=0, keepdims=True)
    return lax.dot_general(side, apart, NN, precision=EXACT, preferred_element_type=f32)


def part_sum(keep_ref, got_ref, mean, side, share, inverse, q):
    size = keep_ref.shape[0] // CYCLES
    rows = pl.ds(q * size, size)
    within = keep_ref[rows, :].astype(f32) + got_ref[rows, :].astype(f32)
    return within * inverse + part_between(mean, side, share)


def part_sums(keep_ref, got_ref, stat_ref, side_ref, share_ref, groups):
    stats = join_stats(stat_ref, got_ref, groups // 2)
    entries = stats.shape[0]
    mean = whole_means(stats)
    size = keep_ref.shape[0] // CYCLES
    return [
        part_sum(
            keep_ref,
            got_ref,
            mean,
            side_ref[pl.ds(q * size, size), :],
            share_ref[pl.ds(q * entries, entries), :][:, :1],
            share_ref[pl.ds(CYCLES * entries + 8 * q, 1), :][:, :1],
            q,
        )
        for q in range(CYCLES)
    ]


def own_part(got, edge):
    groups, tall, width = got.shape
    size = (tall - STAT_ROWS) // CYCLES
    entries = groups * STAT
    outs = [((CYCLES * size, width), f32), ((CYCLES * size, entries), f32), ((CYCLES * (entries + 8), LANE), f32)]
    return kernel_call(functools.partial(own_part_kernel, edge=edge), "own_part", (got,), outs)


def finish_kernel(own_ref, side_ref, share_ref, *refs, parts, rows, edge, groups):
    refs, out_ref = refs[:-1], refs[-1]
    size = out_ref.shape[0]
    mid = rows - 2 * edge
    me = lax.axis_index("frame")
    sums = [[ref[pl.ds(q * size, size), :] for q in range(CYCLES)] for ref in (own_ref,)]
    sums += [part_sums(*refs[i : i + 3], side_ref, share_ref, groups) for i in range(0, len(refs), 3)]
    for q in range(CYCLES):
        for j, ((mid_part, mid_at), (edge_part, edge_at)) in enumerate(parts):
            mids = sums[mid_part][q][:, mid_at : mid_at + mid]
            edges = sums[edge_part][q][:, edge_at : edge_at + 2 * edge]
            natural = jnp.concatenate([edges[:, :edge], mids, edges[:, edge:]], axis=1)
            out_ref[:, q, pl.ds(pl.multiple_of((me ^ j) * rows, rows), rows)] = natural


def swap(x, axis, bit):
    return lax.ppermute(x, axis, [(i, i ^ bit) for i in range(lax.axis_size(axis))])


def swap_pieces(x, n):
    size = x.shape[0] // n
    return [swap(x[i * size : (i + 1) * size], "frame", 1) for i in range(n)]


def shards(frames, dead_time, band_width, cycle_label, valid):
    nblocks = lax.axis_size("frame")
    ngroups = lax.axis_size("pixel")
    rows = frames.shape[0]
    nframes = rows * nblocks
    own_rows = rows // ngroups
    edge_rows = max(rows // EDGE_PART, 32)
    mid_rows = rows - 2 * edge_rows
    chip = lax.axis_index("frame") // 2
    even = lax.axis_index("frame") % 2 == 0

    near_halo, far_halo = halos(frames)
    mid, rim, dead, width = smooth_middle(frames, dead_time, band_width, edge_rows)
    halo = far_halo
    for bit in sorted({x ^ (x + 1) for x in range(nblocks // 2 - 1)}):
        got = swap(far_halo, "frame", 2 * bit)
        wanted = (chip ^ bit) == jnp.where(even, chip + 1, chip - 1)
        halo = got if bit == 1 else jnp.where(wanted, got, halo)
    mid = hold(mid, halo)
    far_mid = {j: swap(mid, "frame", j) for j in range(2, nblocks, 2)}
    near_halo = swap(near_halo, "frame", 1)
    halo = swap(halo, "frame", 1)
    near = swap_pieces(mid, 4)
    edge = smooth_edges(rim, near_halo, halo, dead, width, nframes)
    far_edge = {j: swap(edge, "frame", j) for j in range(2, nblocks, 2)}
    near += swap_pieces(edge, 4)

    def exchange(send, level):
        return swap(send, "pixel", 2**level)

    levels = ngroups.bit_length() - 1
    own, left, total = gram_own(cycle_label, valid, mid, edge, near, ngroups)
    wait = [total]
    own, side, share = own_part(lax.all_to_all(own, "pixel", 0, 0, tiled=True), edge_rows)

    others, places = [], []
    later = []
    for j in range(2, nblocks, 2):
        for source, n in ((far_mid[j], 4), (far_edge[j], 1)):
            source = hold(source, *wait)
            keep, send, stat = gram_cross(left, total, [source, *swap_pieces(source, n)], ngroups)
            wait = [stat]
            for level in range(levels):
                got = exchange(send, level)
                if level + 1 < levels:
                    keep, send, stat = merge(keep, got, stat, 2**level)
            later = [own, send]
            places.append((1 + len(others) // 3, source.shape[0]))
            others += [keep, got, stat]
    parts = [((0, 0), (0, mid_rows)), ((0, rows), (0, rows + mid_rows))]
    for pair in zip(places[::2], places[1::2]):
        parts += [tuple((p, i * n) for p, n in pair) for i in range(2)]
    return kernel_call(
        functools.partial(finish_kernel, parts=parts, rows=rows, edge=edge_rows, groups=ngroups),
        "finish",
        (own, side, share, *others),
        [((own_rows, CYCLES, nframes), f32)],
    )[0]


def solution(mesh):
    in_specs = (P("frame", "pixel"), P("pixel"), P("pixel"), P("pixel"), P("pixel"))
    out_specs = P(("frame", "pixel"), None, None)
    return jax.shard_map(shards, mesh=mesh, in_specs=in_specs, out_specs=out_specs, check_vma=False)
```

```python
import functools
import jax
import jax.numpy as jnp
from jax import lax
from jax.experimental import pallas as pl
from jax.experimental.pallas import tpu as pltpu
from jax.sharding import PartitionSpec as P

CYCLES = 2
BAND = 8
HALO = 16
EDGE_PART = 4
FORWARDS = ((4, 8, 12), (12,), ())
STAT = 8
STAT_ROWS = 8
TURNS = (0, 0)
LANE = 128
f32 = jnp.float32
bf16 = jnp.bfloat16
NT = (((1,), (1,)), ((), ()))
NN = (((1,), (0,)), ((), ()))
EXACT = lax.Precision.HIGHEST


def kernel_call(body, name, args, outs, scratch=(), in_specs=None, mib=4, aliases={}):
    vmem = pl.BlockSpec(memory_space=pltpu.VMEM)
    return pl.pallas_call(
        body,
        in_specs=in_specs or [vmem] * len(args),
        out_specs=[vmem] * len(outs),
        out_shape=[jax.ShapeDtypeStruct(shape, dtype) for shape, dtype in outs],
        scratch_shapes=list(scratch),
        input_output_aliases=aliases,
        compiler_params=pltpu.CompilerParams(vmem_limit_bytes=mib * 2**20),
        cost_estimate=pl.CostEstimate(flops=0, bytes_accessed=2**18, transcendentals=0),
        name=name,
    )(*args)


def correct(raw, dead):
    rate = 4.0 + raw.astype(f32)
    return rate / (1.0 - dead * rate)


def band_sum(c_ref, at, n, width):
    acc = c_ref[pl.ds(at, n), :]
    for k in range(1, BAND + 1):
        pair = c_ref[pl.ds(at - k, n), :] + c_ref[pl.ds(at + k, n), :]
        acc = acc + jnp.where(width >= k, pair, 0.0)
    return acc


def halo_kernel(frames_ref, near_ref, far_ref, ends_ref, sems):
    rows = frames_ref.shape[0]
    copies = [
        pltpu.make_async_copy(frames_ref.at[pl.ds(at, HALO)], ends_ref.at[i], sems.at[i])
        for i, at in enumerate((0, rows - HALO))
    ]
    for copy in copies:
        copy.start()
    for copy in copies:
        copy.wait()
    even = lax.axis_index("frame") % 2 == 0
    first, last = ends_ref[0], ends_ref[1]
    far_ref[...] = jnp.where(even, first, last)
    near_ref[...] = jnp.where(even, last, first)


def halos(frames):
    rows, px = frames.shape
    return kernel_call(
        halo_kernel,
        "halos",
        (frames,),
        [((HALO, px), bf16)] * 2,
        [pltpu.VMEM((2, HALO, px), bf16), pltpu.SemaphoreType.DMA((2,))],
        in_specs=[pl.BlockSpec(memory_space=pltpu.HBM)],
    )


def middle_kernel(frames_ref, dead_hbm, width_hbm, mid_ref, rim_ref, dead_ref, width_ref, raw_ref, c_ref, sems):
    rows, px = frames_ref.shape
    edge = rim_ref.shape[0] // 2 - HALO
    tile = 32
    chunk = min(512, px)
    small = [pltpu.make_async_copy(dead_hbm, dead_ref, sems.at[0]), pltpu.make_async_copy(width_hbm, width_ref, sems.at[1])]
    large = [
        pltpu.make_async_copy(frames_ref.at[:, pl.ds(i * chunk, chunk)], raw_ref.at[:, pl.ds(i * chunk, chunk)], sems.at[2 + i])
        for i in range(px // chunk)
    ]
    for copy in small + large:
        copy.start()
    for copy in small:
        copy.wait()
    for i, copy in enumerate(large):
        copy.wait()
        part = pl.ds(i * chunk, chunk)
        rim_ref[pl.ds(0, edge + HALO), part] = raw_ref[pl.ds(0, edge + HALO), part]
        rim_ref[pl.ds(edge + HALO, edge + HALO), part] = raw_ref[pl.ds(rows - edge - HALO, edge + HALO), part]
        for col in range(chunk // LANE):
            lanes = pl.ds(i * chunk + col * LANE, LANE)
            dead = dead_ref[lanes][None, :]
            width = width_ref[lanes][None, :]
            inverse = 1.0 / (2 * width + 1).astype(f32)
            c_ref[...] = correct(raw_ref[pl.ds(edge - HALO, rows - 2 * edge + 2 * HALO), lanes], dead)
            for r in range((rows - 2 * edge) // tile):
                acc = band_sum(c_ref, HALO + r * tile, tile, width)
                mid_ref[pl.ds(r * tile, tile), lanes] = (acc * inverse).astype(bf16)


def edge_kernel(rim_ref, near_ref, far_ref, dead_ref, width_ref, out_ref, top_ref, bottom_ref, c_ref, *, nframes):
    px = rim_ref.shape[1]
    edge = out_ref.shape[0] // 2
    rows = nframes // lax.axis_size("frame")
    tile = 32
    block = lax.axis_index("frame")
    even = block % 2 == 0
    begin = block * rows
    has_up = (block > 0).astype(f32)
    has_down = ((block + 1) * rows < nframes).astype(f32)
    span = edge + 2 * HALO
    for col in range(px // LANE):
        lanes = pl.ds(col * LANE, LANE)
        dead = dead_ref[lanes][None, :]
        width = width_ref[lanes][None, :]
        near, far = near_ref[:, lanes], far_ref[:, lanes]
        c_ref[pl.ds(0, HALO), :] = correct(jnp.where(even, far, near), dead) * has_up
        c_ref[pl.ds(HALO, edge + HALO), :] = correct(rim_ref[pl.ds(0, edge + HALO), lanes], dead)
        c_ref[pl.ds(span, edge + HALO), :] = correct(rim_ref[pl.ds(edge + HALO, edge + HALO), lanes], dead)
        c_ref[pl.ds(span + edge + HALO, HALO), :] = correct(jnp.where(even, near, far), dead) * has_down
        for half in range(2):
            for r in range(edge // tile):
                acc = band_sum(c_ref, half * span + HALO + r * tile, tile, width)
                first = begin + half * (rows - edge) + r * tile
                t = first + lax.broadcasted_iota(jnp.int32, (tile, LANE), 0)
                terms = jnp.minimum(t + width, nframes - 1) - jnp.maximum(t - width, 0) + 1
                smoothed = (acc / terms.astype(f32)).astype(bf16)
                out_ref[pl.ds(half * edge + r * tile, tile), lanes] = smoothed
                (top_ref, bottom_ref)[half][pl.ds(r * tile, tile), lanes] = smoothed


def smooth_middle(frames, dead, width, edge):
    rows, px = frames.shape
    mid = rows - 2 * edge
    return kernel_call(
        middle_kernel,
        "smooth_middle",
        (frames, dead, width),
        [((mid, px), bf16), ((2 * (edge + HALO), px), bf16), ((px,), f32), ((px,), jnp.int32)],
        [pltpu.VMEM((rows, px), bf16), pltpu.VMEM((mid + 2 * HALO, LANE), f32), pltpu.SemaphoreType.DMA((2 + px // min(512, px),))],
        in_specs=[pl.BlockSpec(memory_space=pltpu.HBM)] * 3,
    )


def smooth_edges(rim, near, far, dead, width, nframes):
    edge = rim.shape[0] // 2 - HALO
    return kernel_call(
        functools.partial(edge_kernel, nframes=nframes),
        "smooth_edges",
        (rim, near, far, dead, width),
        [((2 * edge, rim.shape[1]), bf16)] + [((edge, rim.shape[1]), bf16)] * 2,
        [pltpu.VMEM((2 * (edge + 2 * HALO), LANE), f32)],
    )


def hold_kernel(*refs):
    pass


def hold(x, *tokens):
    anywhere = pl.BlockSpec(memory_space=pl.ANY)
    return pl.pallas_call(
        hold_kernel,
        in_specs=[anywhere] * (1 + len(tokens)),
        out_specs=anywhere,
        out_shape=jax.ShapeDtypeStruct(x.shape, x.dtype),
        input_output_aliases={0: 0},
        compiler_params=pltpu.CompilerParams(vmem_limit_bytes=2**20),
        cost_estimate=pl.CostEstimate(flops=0, bytes_accessed=0, transcendentals=0),
        name="hold",
    )(x, *tokens)


def tree_order(bits):
    return [(high << bits[0]) + slot for high in range(2) for slot in tree_order(bits[1:])] if bits else [0]


def centre(product_ref, total_ref, mean, keep_ref, send_ref, bits):
    rows = product_ref.shape[0] // CYCLES - 16
    half = 2 ** len(bits) // 2
    size = rows // (2 * half)
    me = lax.axis_index("pixel")
    for at, slot in enumerate(tree_order(bits)):
        out_ref = send_ref if at >= half else keep_ref
        place = (at % half) * CYCLES * size
        for q in range(CYCLES):
            begin = pl.multiple_of(q * rows + (me ^ slot) * size, size)
            total = total_ref[pl.ds(begin, size), :]
            for j in range(keep_ref.shape[1] // LANE):
                lanes = pl.ds(j * LANE, LANE)
                centred = product_ref[pl.ds(begin, size), lanes] - total * mean[q][:, j * LANE : (j + 1) * LANE]
                out_ref[pl.ds(place + q * size, size), lanes] = centred.astype(bf16)


def means(product_ref, total_ref, width):
    base = product_ref.shape[0] - 16 * CYCLES
    count = [total_ref[pl.ds(base + 16 * q, 1), :][:, :1] for q in range(CYCLES)]
    mean = [product_ref[pl.ds(base + 16 * q, 1), pl.ds(0, width)] / jnp.maximum(count[q], 1.0) for q in range(CYCLES)]
    return mean, count


def split(x, pieces):
    out = []
    for _ in range(pieces):
        out.append(x.astype(bf16).astype(f32))
        x = x - out[-1]
    return out


def stat_rows(mean, count=None):
    width = mean[0].shape[1]
    rows = [piece for m in zip(*[split(m, 3) for m in mean]) for piece in m]
    zero = jnp.zeros((1, width), f32)
    if count is None:
        rows += [zero] * 2
    else:
        lane = lax.broadcasted_iota(jnp.int32, (1, width), 1) // (LANE // 2)
        for part in zip(*[split(c, 2) for c in count]):
            rows.append(sum(jnp.where(lane == q, p, 0.0) for q, p in enumerate(part)))
    return jnp.concatenate(rows + [zero] * (STAT_ROWS - len(rows)), axis=0).astype(bf16)


def gram_own_kernel(label_ref, valid_ref, mid_ref, edge_ref, *refs, groups):
    near_refs, (out_ref, left_ref, total_ref, acc_ref) = refs[:-4], refs[-4:]
    px = mid_ref.shape[1]
    rim = edge_ref.shape[0] // 2
    rows = mid_ref.shape[0] + 2 * rim
    width = 2 * rows
    label = label_ref[...][None, :]
    used = valid_ref[...][None, :] == 1
    for q in range(CYCLES):
        weight = jnp.broadcast_to(((label == q) & used).astype(f32), (16, px)).astype(bf16)
        left_ref[pl.ds(q * rows, rim), :] = edge_ref[pl.ds(0, rim), :] * weight[:1]
        left_ref[pl.ds(q * rows + rim, rows - 2 * rim), :] = mid_ref[...] * weight[:1]
        left_ref[pl.ds((q + 1) * rows - rim, rim), :] = edge_ref[pl.ds(rim, rim), :] * weight[:1]
        left_ref[pl.ds(CYCLES * rows + 16 * q, 16), :] = weight
    right = jnp.concatenate([ref[...] for ref in (mid_ref, edge_ref, *near_refs)] + [jnp.ones((LANE, px), bf16)], axis=0)
    acc_ref[...] = lax.dot_general(left_ref[...], right, NT, preferred_element_type=f32)
    total_ref[...] = acc_ref[:, pl.ds(width, LANE)]
    mean, count = means(acc_ref, total_ref, width)
    size = rows // groups
    stats = stat_rows(mean, count)
    for group in range(groups):
        for q in range(CYCLES):
            here = pl.ds(q * rows + group * size, size)
            for j in range(width // LANE):
                lanes = pl.ds(j * LANE, LANE)
                centred = acc_ref[here, lanes] - total_ref[here, :] * mean[q][:, j * LANE : (j + 1) * LANE]
                out_ref[group, pl.ds(q * size, size), lanes] = centred.astype(bf16)
        out_ref[group, pl.ds(CYCLES * size, STAT_ROWS), :] = stats


def part_outs(rows, width, stat_rows):
    return [((rows, width), bf16), ((rows + stat_rows, width), bf16), ((stat_rows, width), bf16)]


def gram_own(label, valid, mid, edge, near, groups):
    px = mid.shape[1]
    rows = mid.shape[0] + edge.shape[0]
    tall = CYCLES * (rows + 16)
    return kernel_call(
        functools.partial(gram_own_kernel, groups=groups),
        "gram_own",
        (label, valid, mid, edge, *near),
        [((groups, CYCLES * rows // groups + STAT_ROWS, 2 * rows), bf16), ((tall, px), bf16), ((tall, LANE), f32)],
        [pltpu.VMEM((tall, 2 * rows + LANE), f32)],
        mib=10,
    )


def gram_cross_kernel(left_ref, total_ref, *refs, bits, cols, at):
    keep_ref, send_ref, stat_ref, acc_ref = refs[-4:]
    right = jnp.concatenate([ref[...] for ref in refs[:cols]], axis=0)
    acc_ref[...] = lax.dot_general(left_ref[...], right, NT, preferred_element_type=f32)
    mean, _ = means(acc_ref, total_ref, acc_ref.shape[1])
    here = pl.ds(at, acc_ref.shape[1])
    stats = stat_rows(mean)
    stat_ref[:, here] = stats
    send_ref[pl.ds(send_ref.shape[0] - STAT_ROWS, STAT_ROWS), here] = stats
    centre(acc_ref, total_ref, mean, keep_ref.at[:, here], send_ref.at[:, here], bits)


def gram_cross(left, total, cols, width, at, part, bits):
    tall = left.shape[0]
    return kernel_call(
        functools.partial(gram_cross_kernel, bits=bits, cols=len(cols), at=at),
        "gram_cross",
        (left, total, *cols, *part),
        part_outs(tall // 2 - 16, width, STAT_ROWS),
        [pltpu.VMEM((tall, sum(c.shape[0] for c in cols)), f32)],
        mib=10,
        aliases={2 + len(cols) + i: i for i in range(len(part))},
    )


def join_stats(mine_ref, got_ref, groups):
    mine = mine_ref[...].astype(f32)
    got = got_ref[pl.ds(got_ref.shape[0] - mine.shape[0], mine.shape[0]), :].astype(f32)
    return jnp.concatenate([mine[: groups * STAT], got[: groups * STAT]], axis=0)


def merge_kernel(keep_ref, got_ref, stat_ref, next_keep_ref, next_send_ref, next_stat_ref, *, groups):
    half = next_keep_ref.shape[0]
    total = keep_ref[...].astype(f32) + got_ref[pl.ds(0, 2 * half), :].astype(f32)
    next_keep_ref[...] = total[:half].astype(bf16)
    next_send_ref[pl.ds(0, half), :] = total[half:].astype(bf16)
    stats = join_stats(stat_ref, got_ref, groups).astype(bf16)
    next_stat_ref[...] = stats
    next_send_ref[pl.ds(half, stats.shape[0]), :] = stats


def merge(keep, got, stat, groups):
    outs = part_outs(keep.shape[0] // 2, keep.shape[1], 2 * groups * STAT)
    return kernel_call(functools.partial(merge_kernel, groups=groups), "merge", (keep, got, stat), outs)


def whole_means(stats):
    n = stats.shape[0]
    return stats + pltpu.roll(stats, n - CYCLES, 0) + pltpu.roll(stats, n - 2 * CYCLES, 0)


def own_part_kernel(got_ref, out_ref, side_ref, share_ref, *, edge):
    groups, _, width = got_ref.shape
    size = out_ref.shape[0] // CYCLES
    rows = width // 2
    mid = rows - 2 * edge
    me = lax.axis_index("pixel")
    stats = [got_ref[me ^ i, pl.ds(CYCLES * size, STAT), :].astype(f32) for i in range(groups)]
    stats = jnp.concatenate(stats, axis=0)
    entries = stats.shape[0]
    kind = lax.broadcasted_iota(jnp.int32, (entries, 1), 0) % STAT
    n = me * size + lax.broadcasted_iota(jnp.int32, (size, rows), 0)
    packed = jnp.where(n < edge, n + mid, jnp.where(n < edge + mid, n - edge, n))
    pick = (packed == lax.broadcasted_iota(jnp.int32, (size, rows), 1)).astype(f32)
    counted = stats + pltpu.roll(stats, entries - 1, 0)
    mean = whole_means(stats)
    for q in range(CYCLES):
        number = pltpu.roll(counted, entries - 3 * CYCLES + q, 0)[:, q * LANE // 2 : q * LANE // 2 + 1]
        number = jnp.where(kind == q, number, 0.0)
        count = jnp.sum(number, axis=0, keepdims=True)
        share = number / count
        share_ref[pl.ds(q * entries, entries), :] = jnp.broadcast_to(share, (entries, LANE))
        share_ref[pl.ds(CYCLES * entries + 8 * q, 8), :] = jnp.broadcast_to(1.0 / count, (8, LANE))
        apart = mean[:, :rows] - jnp.sum(mean[:, :rows] * share, axis=0, keepdims=True)
        side = lax.dot_general(pick, apart * share, NT, precision=EXACT, preferred_element_type=f32)
        here = pl.ds(q * size, size)
        side_ref[here, :] = side
        within = got_ref[0, here, :].astype(f32)
        for group in range(1, groups):
            within += got_ref[group, here, :].astype(f32)
        out_ref[here, :] = within * (1.0 / count) + part_between(mean, side, share)


def part_between(mean, side, share):
    apart = mean - jnp.sum(mean * share, axis=0, keepdims=True)
    return lax.dot_general(side, apart, NN, precision=EXACT, preferred_element_type=f32)


def part_sum(keep_ref, got_ref, mean, side, share, inverse, q):
    size = keep_ref.shape[0] // CYCLES
    rows = pl.ds(q * size, size)
    within = keep_ref[rows, :].astype(f32) + got_ref[rows, :].astype(f32)
    return within * inverse + part_between(mean, side, share)


def part_sums(keep_ref, got_ref, stat_ref, side_ref, share_ref, bits):
    stats = join_stats(stat_ref, got_ref, 2 ** len(bits) // 2)
    spots = [sum((group >> bit & 1) << level for level, bit in enumerate(bits)) for group in range(2 ** len(bits))]
    stats = jnp.concatenate([stats[STAT * spot : STAT * (spot + 1)] for spot in spots], axis=0)
    entries = stats.shape[0]
    mean = whole_means(stats)
    size = keep_ref.shape[0] // CYCLES
    return [
        part_sum(
            keep_ref,
            got_ref,
            mean,
            side_ref[pl.ds(q * size, size), :],
            share_ref[pl.ds(q * entries, entries), :][:, :1],
            share_ref[pl.ds(CYCLES * entries + 8 * q, 1), :][:, :1],
            q,
        )
        for q in range(CYCLES)
    ]


def own_part(got, edge):
    groups, tall, width = got.shape
    size = (tall - STAT_ROWS) // CYCLES
    entries = groups * STAT
    outs = [((CYCLES * size, width), f32), ((CYCLES * size, entries), f32), ((CYCLES * (entries + 8), LANE), f32)]
    return kernel_call(functools.partial(own_part_kernel, edge=edge), "own_part", (got,), outs)


def finish_kernel(own_ref, side_ref, share_ref, *refs, parts, rows, edge, orders):
    refs, out_ref = refs[:-1], refs[-1]
    size = out_ref.shape[0]
    mid = rows - 2 * edge
    me = lax.axis_index("frame")
    sums = [[ref[pl.ds(q * size, size), :] for q in range(CYCLES)] for ref in (own_ref,)]
    sums += [part_sums(*refs[i : i + 3], side_ref, share_ref, orders[i // 3 % 2]) for i in range(0, len(refs), 3)]
    for q in range(CYCLES):
        for j, places in enumerate(parts):
            pieces = [sums[part][q][:, at : at + n] for (part, at), n in zip(places, (mid, edge, edge))]
            natural = jnp.concatenate([pieces[1], pieces[0], pieces[2]], axis=1)
            out_ref[:, q, pl.ds(pl.multiple_of((me ^ j) * rows, rows), rows)] = natural


def swap(x, axis, bit):
    return lax.ppermute(x, axis, [(i, i ^ bit) for i in range(lax.axis_size(axis))])


def swap_pieces(x, *cuts):
    at = [0] + [x.shape[0] * cut // 16 for cut in cuts] + [x.shape[0]]
    return [swap(x[i:j], "frame", 1) for i, j in zip(at, at[1:])]


def shards(frames, dead_time, band_width, cycle_label, valid):
    nblocks = lax.axis_size("frame")
    ngroups = lax.axis_size("pixel")
    rows = frames.shape[0]
    nframes = rows * nblocks
    own_rows = rows // ngroups
    edge_rows = max(rows // EDGE_PART, 32)
    mid_rows = rows - 2 * edge_rows
    chip = lax.axis_index("frame") // 2
    even = lax.axis_index("frame") % 2 == 0

    near_halo, far_halo = halos(frames)
    mid, rim, dead, width = smooth_middle(frames, dead_time, band_width, edge_rows)
    halo = far_halo
    for bit in sorted({x ^ (x + 1) for x in range(nblocks // 2 - 1)}):
        got = swap(far_halo, "frame", 2 * bit)
        wanted = (chip ^ bit) == jnp.where(even, chip + 1, chip - 1)
        halo = got if bit == 1 else jnp.where(wanted, got, halo)
    mid = hold(mid, halo)
    far_mid = {j: swap(mid, "frame", j) for j in range(2, nblocks, 2)}
    near_halo = swap(near_halo, "frame", 1)
    halo = swap(halo, "frame", 1)
    near = swap_pieces(mid, 8)
    edge, top, bottom = smooth_edges(rim, near_halo, halo, dead, width, nframes)
    far_ends = {j: [swap(x, "frame", j) for x in (top, bottom)] for j in range(2, nblocks, 2)}
    near += swap_pieces(edge, 8)

    levels = ngroups.bit_length() - 1
    orders = [tuple((level + turn) % levels for level in range(levels)) for turn in TURNS]
    own, left, total = gram_own(cycle_label, valid, mid, edge, near, ngroups)
    wait = [total]
    own, side, share = own_part(lax.all_to_all(own, "pixel", 0, 0, tiled=True), edge_rows)

    sizes = (mid_rows, edge_rows, edge_rows)
    split = [[(0,)], [(1,), (2,)] if 2 * edge_rows % LANE == 0 else [(1, 2)]]
    others = []
    parts = [[(0, i * rows), (0, i * rows + mid_rows), (0, i * rows + mid_rows + edge_rows)] for i in range(2)]
    for j in range(2, nblocks, 2):
        places = [[None] * 3, [None] * 3]
        pieces = [far_mid[j], *far_ends[j]]
        for part in split:
            width = 2 * sum(sizes[k] for group in part for k in group)
            at, done = 0, ()
            bits = orders[len(others) // 3 % 2]
            for group in part:
                group_rows = sum(sizes[k] for k in group)
                far, near = [], []
                for k in group:
                    for i in range(2):
                        places[i][k] = (1 + len(others) // 3, at + i * group_rows + sum(x.shape[0] for x in far))
                    far.append(hold(pieces[k], *wait))
                    near += swap_pieces(far[-1], *FORWARDS[k])
                done = gram_cross(left, total, far + near, width, at, done, bits)
                at += 2 * group_rows
                wait = [done[2]]
            keep, send, stat = done
            for level in range(levels):
                got = swap(send, "pixel", 1 << bits[level])
                if level + 1 < levels:
                    keep, send, stat = merge(keep, got, stat, 2**level)
            others += [keep, got, stat]
        parts += places
    return kernel_call(
        functools.partial(finish_kernel, parts=parts, rows=rows, edge=edge_rows, orders=orders),
        "finish",
        (own, side, share, *others),
        [((own_rows, CYCLES, nframes), f32)],
    )[0]


def solution(mesh):
    in_specs = (P("frame", "pixel"), P("pixel"), P("pixel"), P("pixel"), P("pixel"))
    out_specs = P(("frame", "pixel"), None, None)
    return jax.shard_map(shards, mesh=mesh, in_specs=in_specs, out_specs=out_specs, check_vma=False)
```

```python
import functools
import jax
import jax.numpy as jnp
from jax import lax
from jax.experimental import pallas as pl
from jax.experimental.pallas import tpu as pltpu
from jax.sharding import PartitionSpec as P

CYCLES = 2
BAND = 8
HALO = 16
EDGE_PART = 4
FORWARDS = ((4, 8, 12), (12,), ())
STAT = 8
STAT_ROWS = 8
LANE = 128
f32 = jnp.float32
bf16 = jnp.bfloat16
NT = (((1,), (1,)), ((), ()))
NN = (((1,), (0,)), ((), ()))
EXACT = lax.Precision.HIGHEST


def kernel_call(body, name, args, outs, scratch=(), in_specs=None, mib=4, aliases={}):
    vmem = pl.BlockSpec(memory_space=pltpu.VMEM)
    return pl.pallas_call(
        body,
        in_specs=in_specs or [vmem] * len(args),
        out_specs=[vmem] * len(outs),
        out_shape=[jax.ShapeDtypeStruct(shape, dtype) for shape, dtype in outs],
        scratch_shapes=list(scratch),
        input_output_aliases=aliases,
        compiler_params=pltpu.CompilerParams(vmem_limit_bytes=mib * 2**20),
        cost_estimate=pl.CostEstimate(flops=0, bytes_accessed=2**18, transcendentals=0),
        name=name,
    )(*args)


def correct(raw, dead):
    rate = 4.0 + raw.astype(f32)
    return rate / (1.0 - dead * rate)


def band_sum(c_ref, at, n, width):
    acc = c_ref[pl.ds(at, n), :]
    for k in range(1, BAND + 1):
        pair = c_ref[pl.ds(at - k, n), :] + c_ref[pl.ds(at + k, n), :]
        acc = acc + jnp.where(width >= k, pair, 0.0)
    return acc


def halo_kernel(frames_ref, near_ref, far_ref):
    rows = frames_ref.shape[0]
    even = lax.axis_index("frame") % 2 == 0
    first, last = frames_ref[pl.ds(0, HALO), :], frames_ref[pl.ds(rows - HALO, HALO), :]
    far_ref[...] = jnp.where(even, first, last)
    near_ref[...] = jnp.where(even, last, first)


def halos(frames):
    px = frames.shape[1]
    return kernel_call(halo_kernel, "halos", (frames,), [((HALO, px), bf16)] * 2)


def middle_kernel(frames_ref, dead_ref, width_ref, mid_ref, rim_ref, c_ref):
    rows, px = frames_ref.shape
    edge = rim_ref.shape[0] // 2 - HALO
    tile = 32
    rim_ref[pl.ds(0, edge + HALO), :] = frames_ref[pl.ds(0, edge + HALO), :]
    rim_ref[pl.ds(edge + HALO, edge + HALO), :] = frames_ref[pl.ds(rows - edge - HALO, edge + HALO), :]
    for col in range(px // LANE):
        lanes = pl.ds(col * LANE, LANE)
        dead = dead_ref[lanes][None, :]
        width = width_ref[lanes][None, :]
        inverse = 1.0 / (2 * width + 1).astype(f32)
        c_ref[...] = correct(frames_ref[pl.ds(edge - HALO, rows - 2 * edge + 2 * HALO), lanes], dead)
        for r in range((rows - 2 * edge) // tile):
            acc = band_sum(c_ref, HALO + r * tile, tile, width)
            mid_ref[pl.ds(r * tile, tile), lanes] = (acc * inverse).astype(bf16)


def edge_kernel(rim_ref, near_ref, far_ref, dead_ref, width_ref, out_ref, top_ref, bottom_ref, c_ref, *, nframes):
    px = rim_ref.shape[1]
    edge = out_ref.shape[0] // 2
    rows = nframes // lax.axis_size("frame")
    tile = 32
    block = lax.axis_index("frame")
    even = block % 2 == 0
    begin = block * rows
    has_up = (block > 0).astype(f32)
    has_down = ((block + 1) * rows < nframes).astype(f32)
    span = edge + 2 * HALO
    for col in range(px // LANE):
        lanes = pl.ds(col * LANE, LANE)
        dead = dead_ref[lanes][None, :]
        width = width_ref[lanes][None, :]
        near, far = near_ref[:, lanes], far_ref[:, lanes]
        c_ref[pl.ds(0, HALO), :] = correct(jnp.where(even, far, near), dead) * has_up
        c_ref[pl.ds(HALO, edge + HALO), :] = correct(rim_ref[pl.ds(0, edge + HALO), lanes], dead)
        c_ref[pl.ds(span, edge + HALO), :] = correct(rim_ref[pl.ds(edge + HALO, edge + HALO), lanes], dead)
        c_ref[pl.ds(span + edge + HALO, HALO), :] = correct(jnp.where(even, near, far), dead) * has_down
        for half in range(2):
            for r in range(edge // tile):
                acc = band_sum(c_ref, half * span + HALO + r * tile, tile, width)
                first = begin + half * (rows - edge) + r * tile
                t = first + lax.broadcasted_iota(jnp.int32, (tile, LANE), 0)
                terms = jnp.minimum(t + width, nframes - 1) - jnp.maximum(t - width, 0) + 1
                smoothed = (acc / terms.astype(f32)).astype(bf16)
                out_ref[pl.ds(half * edge + r * tile, tile), lanes] = smoothed
                (top_ref, bottom_ref)[half][pl.ds(r * tile, tile), lanes] = smoothed


def smooth_middle(frames, dead, width, edge):
    rows, px = frames.shape
    mid = rows - 2 * edge
    return kernel_call(
        middle_kernel,
        "smooth_middle",
        (frames, dead, width),
        [((mid, px), bf16), ((2 * (edge + HALO), px), bf16)],
        [pltpu.VMEM((mid + 2 * HALO, LANE), f32)],
    )


def smooth_edges(rim, near, far, dead, width, nframes):
    edge = rim.shape[0] // 2 - HALO
    return kernel_call(
        functools.partial(edge_kernel, nframes=nframes),
        "smooth_edges",
        (rim, near, far, dead, width),
        [((2 * edge, rim.shape[1]), bf16)] + [((edge, rim.shape[1]), bf16)] * 2,
        [pltpu.VMEM((2 * (edge + 2 * HALO), LANE), f32)],
    )


def hold_kernel(*refs):
    pass


def hold(x, *tokens):
    anywhere = pl.BlockSpec(memory_space=pl.ANY)
    return pl.pallas_call(
        hold_kernel,
        in_specs=[anywhere] * (1 + len(tokens)),
        out_specs=anywhere,
        out_shape=jax.ShapeDtypeStruct(x.shape, x.dtype),
        input_output_aliases={0: 0},
        compiler_params=pltpu.CompilerParams(vmem_limit_bytes=2**20),
        cost_estimate=pl.CostEstimate(flops=0, bytes_accessed=0, transcendentals=0),
        name="hold",
    )(x, *tokens)


def tree_order(bits):
    return [(high << bits[0]) + slot for high in range(2) for slot in tree_order(bits[1:])] if bits else [0]


def centre(product_ref, total_ref, mean, keep_ref, send_ref, bits):
    rows = product_ref.shape[0] // CYCLES - 16
    half = 2 ** len(bits) // 2
    size = rows // (2 * half)
    me = lax.axis_index("pixel")
    for at, slot in enumerate(tree_order(bits)):
        out_ref = send_ref if at >= half else keep_ref
        place = (at % half) * CYCLES * size
        for q in range(CYCLES):
            begin = pl.multiple_of(q * rows + (me ^ slot) * size, size)
            total = total_ref[pl.ds(begin, size), :]
            for j in range(keep_ref.shape[1] // LANE):
                lanes = pl.ds(j * LANE, LANE)
                centred = product_ref[pl.ds(begin, size), lanes] - total * mean[q][:, j * LANE : (j + 1) * LANE]
                out_ref[pl.ds(place + q * size, size), lanes] = centred.astype(bf16)


def means(product_ref, total_ref, width):
    base = product_ref.shape[0] - 16 * CYCLES
    count = [total_ref[pl.ds(base + 16 * q, 1), :][:, :1] for q in range(CYCLES)]
    mean = [product_ref[pl.ds(base + 16 * q, 1), pl.ds(0, width)] / jnp.maximum(count[q], 1.0) for q in range(CYCLES)]
    return mean, count


def split(x, pieces):
    out = []
    for _ in range(pieces):
        out.append(x.astype(bf16).astype(f32))
        x = x - out[-1]
    return out


def stat_rows(mean, count=None):
    width = mean[0].shape[1]
    rows = [piece for m in zip(*[split(m, 3) for m in mean]) for piece in m]
    zero = jnp.zeros((1, width), f32)
    if count is None:
        rows += [zero] * 2
    else:
        lane = lax.broadcasted_iota(jnp.int32, (1, width), 1) // (LANE // 2)
        for part in zip(*[split(c, 2) for c in count]):
            rows.append(sum(jnp.where(lane == q, p, 0.0) for q, p in enumerate(part)))
    return jnp.concatenate(rows + [zero] * (STAT_ROWS - len(rows)), axis=0).astype(bf16)


def gram_own_kernel(label_ref, valid_ref, mid_ref, edge_ref, *refs, groups):
    near_refs, (out_ref, left_ref, total_ref, acc_ref) = refs[:-4], refs[-4:]
    px = mid_ref.shape[1]
    rim = edge_ref.shape[0] // 2
    rows = mid_ref.shape[0] + 2 * rim
    width = 2 * rows
    label = label_ref[...][None, :]
    used = valid_ref[...][None, :] == 1
    for q in range(CYCLES):
        weight = jnp.broadcast_to(((label == q) & used).astype(f32), (16, px)).astype(bf16)
        left_ref[pl.ds(q * rows, rim), :] = edge_ref[pl.ds(0, rim), :] * weight[:1]
        left_ref[pl.ds(q * rows + rim, rows - 2 * rim), :] = mid_ref[...] * weight[:1]
        left_ref[pl.ds((q + 1) * rows - rim, rim), :] = edge_ref[pl.ds(rim, rim), :] * weight[:1]
        left_ref[pl.ds(CYCLES * rows + 16 * q, 16), :] = weight
    right = jnp.concatenate([ref[...] for ref in (mid_ref, edge_ref, *near_refs)] + [jnp.ones((LANE, px), bf16)], axis=0)
    acc_ref[...] = lax.dot_general(left_ref[...], right, NT, preferred_element_type=f32)
    total_ref[...] = acc_ref[:, pl.ds(width, LANE)]
    mean, count = means(acc_ref, total_ref, width)
    size = rows // groups
    stats = stat_rows(mean, count)
    for group in range(groups):
        for q in range(CYCLES):
            here = pl.ds(q * rows + group * size, size)
            for j in range(width // LANE):
                lanes = pl.ds(j * LANE, LANE)
                centred = acc_ref[here, lanes] - total_ref[here, :] * mean[q][:, j * LANE : (j + 1) * LANE]
                out_ref[group, pl.ds(q * size, size), lanes] = centred.astype(bf16)
        out_ref[group, pl.ds(CYCLES * size, STAT_ROWS), :] = stats


def part_outs(rows, width, stat_rows):
    return [((rows, width), bf16), ((rows + stat_rows, width), bf16), ((stat_rows, width), bf16)]


def gram_own(label, valid, mid, edge, near, groups):
    px = mid.shape[1]
    rows = mid.shape[0] + edge.shape[0]
    tall = CYCLES * (rows + 16)
    return kernel_call(
        functools.partial(gram_own_kernel, groups=groups),
        "gram_own",
        (label, valid, mid, edge, *near),
        [((groups, CYCLES * rows // groups + STAT_ROWS, 2 * rows), bf16), ((tall, px), bf16), ((tall, LANE), f32)],
        [pltpu.VMEM((tall, 2 * rows + LANE), f32)],
        mib=10,
    )


def gram_cross_kernel(left_ref, total_ref, *refs, bits, cols, at):
    keep_ref, send_ref, stat_ref, acc_ref = refs[-4:]
    right = jnp.concatenate([ref[...] for ref in refs[:cols]], axis=0)
    acc_ref[...] = lax.dot_general(left_ref[...], right, NT, preferred_element_type=f32)
    mean, _ = means(acc_ref, total_ref, acc_ref.shape[1])
    here = pl.ds(at, acc_ref.shape[1])
    stats = stat_rows(mean)
    stat_ref[:, here] = stats
    send_ref[pl.ds(send_ref.shape[0] - STAT_ROWS, STAT_ROWS), here] = stats
    centre(acc_ref, total_ref, mean, keep_ref.at[:, here], send_ref.at[:, here], bits)


def gram_cross(left, total, cols, width, at, part, bits):
    tall = left.shape[0]
    return kernel_call(
        functools.partial(gram_cross_kernel, bits=bits, cols=len(cols), at=at),
        "gram_cross",
        (left, total, *cols, *part),
        part_outs(tall // 2 - 16, width, STAT_ROWS),
        [pltpu.VMEM((tall, sum(c.shape[0] for c in cols)), f32)],
        mib=10,
        aliases={2 + len(cols) + i: i for i in range(len(part))},
    )


def join_stats(mine_ref, got_ref, groups):
    mine = mine_ref[...].astype(f32)
    got = got_ref[pl.ds(got_ref.shape[0] - mine.shape[0], mine.shape[0]), :].astype(f32)
    return jnp.concatenate([mine[: groups * STAT], got[: groups * STAT]], axis=0)


def merge_kernel(keep_ref, got_ref, stat_ref, next_keep_ref, next_send_ref, next_stat_ref, *, groups):
    half = next_keep_ref.shape[0]
    total = keep_ref[...].astype(f32) + got_ref[pl.ds(0, 2 * half), :].astype(f32)
    next_keep_ref[...] = total[:half].astype(bf16)
    next_send_ref[pl.ds(0, half), :] = total[half:].astype(bf16)
    stats = join_stats(stat_ref, got_ref, groups).astype(bf16)
    next_stat_ref[...] = stats
    next_send_ref[pl.ds(half, stats.shape[0]), :] = stats


def merge(keep, got, stat, groups):
    outs = part_outs(keep.shape[0] // 2, keep.shape[1], 2 * groups * STAT)
    return kernel_call(functools.partial(merge_kernel, groups=groups), "merge", (keep, got, stat), outs)


def whole_means(stats):
    n = stats.shape[0]
    return stats + pltpu.roll(stats, n - CYCLES, 0) + pltpu.roll(stats, n - 2 * CYCLES, 0)


def own_part_kernel(got_ref, out_ref, side_ref, share_ref, *, edge):
    groups, _, width = got_ref.shape
    size = out_ref.shape[0] // CYCLES
    rows = width // 2
    mid = rows - 2 * edge
    me = lax.axis_index("pixel")
    stats = [got_ref[me ^ i, pl.ds(CYCLES * size, STAT), :].astype(f32) for i in range(groups)]
    stats = jnp.concatenate(stats, axis=0)
    entries = stats.shape[0]
    kind = lax.broadcasted_iota(jnp.int32, (entries, 1), 0) % STAT
    n = me * size + lax.broadcasted_iota(jnp.int32, (size, rows), 0)
    packed = jnp.where(n < edge, n + mid, jnp.where(n < edge + mid, n - edge, n))
    pick = (packed == lax.broadcasted_iota(jnp.int32, (size, rows), 1)).astype(f32)
    counted = stats + pltpu.roll(stats, entries - 1, 0)
    mean = whole_means(stats)
    for q in range(CYCLES):
        number = pltpu.roll(counted, entries - 3 * CYCLES + q, 0)[:, q * LANE // 2 : q * LANE // 2 + 1]
        number = jnp.where(kind == q, number, 0.0)
        count = jnp.sum(number, axis=0, keepdims=True)
        share = number / count
        share_ref[pl.ds(q * entries, entries), :] = jnp.broadcast_to(share, (entries, LANE))
        share_ref[pl.ds(CYCLES * entries + 8 * q, 8), :] = jnp.broadcast_to(1.0 / count, (8, LANE))
        apart = mean[:, :rows] - jnp.sum(mean[:, :rows] * share, axis=0, keepdims=True)
        side = lax.dot_general(pick, apart * share, NT, precision=EXACT, preferred_element_type=f32)
        here = pl.ds(q * size, size)
        side_ref[here, :] = side
        within = got_ref[0, here, :].astype(f32)
        for group in range(1, groups):
            within += got_ref[group, here, :].astype(f32)
        out_ref[here, :] = within * (1.0 / count) + part_between(mean, side, share)


def part_between(mean, side, share):
    apart = mean - jnp.sum(mean * share, axis=0, keepdims=True)
    return lax.dot_general(side, apart, NN, precision=EXACT, preferred_element_type=f32)


def part_sum(keep_ref, got_ref, mean, side, share, inverse, q):
    size = keep_ref.shape[0] // CYCLES
    rows = pl.ds(q * size, size)
    within = keep_ref[rows, :].astype(f32) + got_ref[rows, :].astype(f32)
    return within * inverse + part_between(mean, side, share)


def part_sums(keep_ref, got_ref, stat_ref, side_ref, share_ref, bits):
    stats = join_stats(stat_ref, got_ref, 2 ** len(bits) // 2)
    spots = [sum((group >> bit & 1) << level for level, bit in enumerate(bits)) for group in range(2 ** len(bits))]
    stats = jnp.concatenate([stats[STAT * spot : STAT * (spot + 1)] for spot in spots], axis=0)
    entries = stats.shape[0]
    mean = whole_means(stats)
    size = keep_ref.shape[0] // CYCLES
    return [
        part_sum(
            keep_ref,
            got_ref,
            mean,
            side_ref[pl.ds(q * size, size), :],
            share_ref[pl.ds(q * entries, entries), :][:, :1],
            share_ref[pl.ds(CYCLES * entries + 8 * q, 1), :][:, :1],
            q,
        )
        for q in range(CYCLES)
    ]


def own_part(got, edge):
    groups, tall, width = got.shape
    size = (tall - STAT_ROWS) // CYCLES
    entries = groups * STAT
    outs = [((CYCLES * size, width), f32), ((CYCLES * size, entries), f32), ((CYCLES * (entries + 8), LANE), f32)]
    return kernel_call(functools.partial(own_part_kernel, edge=edge), "own_part", (got,), outs)


def finish_kernel(own_ref, side_ref, share_ref, *refs, parts, rows, edge, orders):
    refs, out_ref = refs[:-1], refs[-1]
    size = out_ref.shape[0]
    mid = rows - 2 * edge
    me = lax.axis_index("frame")
    sums = [[ref[pl.ds(q * size, size), :] for q in range(CYCLES)] for ref in (own_ref,)]
    sums += [part_sums(*refs[i : i + 3], side_ref, share_ref, orders[i // 3 % 2]) for i in range(0, len(refs), 3)]
    for q in range(CYCLES):
        for j, places in enumerate(parts):
            pieces = [sums[part][q][:, at : at + n] for (part, at), n in zip(places, (mid, edge, edge))]
            natural = jnp.concatenate([pieces[1], pieces[0], pieces[2]], axis=1)
            out_ref[:, q, pl.ds(pl.multiple_of((me ^ j) * rows, rows), rows)] = natural


def swap(x, axis, bit):
    return lax.ppermute(x, axis, [(i, i ^ bit) for i in range(lax.axis_size(axis))])


def swap_pieces(x, *cuts):
    at = [0] + [x.shape[0] * cut // 16 for cut in cuts] + [x.shape[0]]
    return [swap(x[i:j], "frame", 1) for i, j in zip(at, at[1:])]


def shards(frames, dead_time, band_width, cycle_label, valid):
    nblocks = lax.axis_size("frame")
    ngroups = lax.axis_size("pixel")
    rows = frames.shape[0]
    nframes = rows * nblocks
    own_rows = rows // ngroups
    edge_rows = max(rows // EDGE_PART, 32)
    mid_rows = rows - 2 * edge_rows
    chip = lax.axis_index("frame") // 2
    even = lax.axis_index("frame") % 2 == 0

    near_halo, far_halo = halos(frames)
    mid, rim = smooth_middle(frames, dead_time, band_width, edge_rows)
    halo = far_halo
    for bit in sorted({x ^ (x + 1) for x in range(nblocks // 2 - 1)}):
        got = swap(far_halo, "frame", 2 * bit)
        wanted = (chip ^ bit) == jnp.where(even, chip + 1, chip - 1)
        halo = got if bit == 1 else jnp.where(wanted, got, halo)
    mid = hold(mid, halo)
    far_mid = {j: swap(mid, "frame", j) for j in range(2, nblocks, 2)}
    near_halo = swap(near_halo, "frame", 1)
    halo = swap(halo, "frame", 1)
    near = swap_pieces(mid, 8)
    edge, top, bottom = smooth_edges(rim, near_halo, halo, dead_time, band_width, nframes)
    far_ends = {j: [swap(x, "frame", j) for x in (top, bottom)] for j in range(2, nblocks, 2)}
    near += swap_pieces(edge, 8)

    levels = ngroups.bit_length() - 1
    straight = tuple(range(levels))
    orders = [straight, (straight[:2][::-1] + straight[2:])]
    own, left, total = gram_own(cycle_label, valid, mid, edge, near, ngroups)
    wait = [total]
    own, side, share = own_part(lax.all_to_all(own, "pixel", 0, 0, tiled=True), edge_rows)

    sizes = (mid_rows, edge_rows, edge_rows)
    split = [[(0,)], [(1,), (2,)] if 2 * edge_rows % LANE == 0 else [(1, 2)]]
    others = []
    parts = [[(0, i * rows), (0, i * rows + mid_rows), (0, i * rows + mid_rows + edge_rows)] for i in range(2)]
    for j in range(2, nblocks, 2):
        places = [[None] * 3, [None] * 3]
        pieces = [far_mid[j], *far_ends[j]]
        for part in split:
            width = 2 * sum(sizes[k] for group in part for k in group)
            at, done = 0, ()
            bits = orders[len(others) // 3 % 2]
            for group in part:
                group_rows = sum(sizes[k] for k in group)
                far, near = [], []
                for k in group:
                    for i in range(2):
                        places[i][k] = (1 + len(others) // 3, at + i * group_rows + sum(x.shape[0] for x in far))
                    far.append(hold(pieces[k], *wait))
                    near += swap_pieces(far[-1], *FORWARDS[k])
                done = gram_cross(left, total, far + near, width, at, done, bits)
                at += 2 * group_rows
                wait = [done[2]]
            keep, send, stat = done
            for level in range(levels):
                got = swap(send, "pixel", 1 << bits[level])
                if level + 1 < levels:
                    keep, send, stat = merge(keep, got, stat, 2**level)
            others += [keep, got, stat]
        parts += places
    return kernel_call(
        functools.partial(finish_kernel, parts=parts, rows=rows, edge=edge_rows, orders=orders),
        "finish",
        (own, side, share, *others),
        [((own_rows, CYCLES, nframes), f32)],
    )[0]


def solution(mesh):
    in_specs = (P("frame", "pixel"), P("pixel"), P("pixel"), P("pixel"), P("pixel"))
    out_specs = P(("frame", "pixel"), None, None)
    return jax.shard_map(shards, mesh=mesh, in_specs=in_specs, out_specs=out_specs, check_vma=False)
```

```python
import functools
import jax
import jax.numpy as jnp
from jax import lax
from jax.experimental import pallas as pl
from jax.experimental.pallas import tpu as pltpu
from jax.sharding import PartitionSpec as P

CYCLES = 2
BAND = 8
HALO = 16
EDGE_PART = 4
FORWARDS = ((4, 8, 12), (12,), ())
STAT = 8
SENT = 4
STAT_ROWS = 8
LANE = 128
f32 = jnp.float32
bf16 = jnp.bfloat16
NT = (((1,), (1,)), ((), ()))
NN = (((1,), (0,)), ((), ()))
EXACT = lax.Precision.HIGHEST


def kernel_call(body, name, args, outs, scratch=(), in_specs=None, mib=4, aliases={}):
    vmem = pl.BlockSpec(memory_space=pltpu.VMEM)
    return pl.pallas_call(
        body,
        in_specs=in_specs or [vmem] * len(args),
        out_specs=[vmem] * len(outs),
        out_shape=[jax.ShapeDtypeStruct(shape, dtype) for shape, dtype in outs],
        scratch_shapes=list(scratch),
        input_output_aliases=aliases,
        compiler_params=pltpu.CompilerParams(vmem_limit_bytes=mib * 2**20),
        cost_estimate=pl.CostEstimate(flops=0, bytes_accessed=2**18, transcendentals=0),
        name=name,
    )(*args)


def correct(raw, dead):
    rate = 4.0 + raw.astype(f32)
    return rate / (1.0 - dead * rate)


def band_sum(c_ref, at, n, width):
    acc = c_ref[pl.ds(at, n), :]
    for k in range(1, BAND + 1):
        pair = c_ref[pl.ds(at - k, n), :] + c_ref[pl.ds(at + k, n), :]
        acc = acc + jnp.where(width >= k, pair, 0.0)
    return acc


def halo_kernel(frames_ref, near_ref, far_ref):
    rows = frames_ref.shape[0]
    even = lax.axis_index("frame") % 2 == 0
    first, last = frames_ref[pl.ds(0, HALO), :], frames_ref[pl.ds(rows - HALO, HALO), :]
    far_ref[...] = jnp.where(even, first, last)
    near_ref[...] = jnp.where(even, last, first)


def halos(frames):
    px = frames.shape[1]
    return kernel_call(halo_kernel, "halos", (frames,), [((HALO, px), bf16)] * 2)


def middle_kernel(frames_ref, dead_ref, width_ref, mid_ref, rim_ref, c_ref):
    rows, px = frames_ref.shape
    edge = rim_ref.shape[0] // 2 - HALO
    tile = 32
    rim_ref[pl.ds(0, edge + HALO), :] = frames_ref[pl.ds(0, edge + HALO), :]
    rim_ref[pl.ds(edge + HALO, edge + HALO), :] = frames_ref[pl.ds(rows - edge - HALO, edge + HALO), :]
    for col in range(px // LANE):
        lanes = pl.ds(col * LANE, LANE)
        dead = dead_ref[lanes][None, :]
        width = width_ref[lanes][None, :]
        inverse = 1.0 / (2 * width + 1).astype(f32)
        c_ref[...] = correct(frames_ref[pl.ds(edge - HALO, rows - 2 * edge + 2 * HALO), lanes], dead)
        for r in range((rows - 2 * edge) // tile):
            acc = band_sum(c_ref, HALO + r * tile, tile, width)
            mid_ref[pl.ds(r * tile, tile), lanes] = (acc * inverse).astype(bf16)


def edge_kernel(rim_ref, near_ref, far_ref, dead_ref, width_ref, out_ref, top_ref, bottom_ref, c_ref, *, nframes):
    px = rim_ref.shape[1]
    edge = out_ref.shape[0] // 2
    rows = nframes // lax.axis_size("frame")
    tile = 32
    block = lax.axis_index("frame")
    even = block % 2 == 0
    begin = block * rows
    has_up = (block > 0).astype(f32)
    has_down = ((block + 1) * rows < nframes).astype(f32)
    span = edge + 2 * HALO
    for col in range(px // LANE):
        lanes = pl.ds(col * LANE, LANE)
        dead = dead_ref[lanes][None, :]
        width = width_ref[lanes][None, :]
        near, far = near_ref[:, lanes], far_ref[:, lanes]
        c_ref[pl.ds(0, HALO), :] = correct(jnp.where(even, far, near), dead) * has_up
        c_ref[pl.ds(HALO, edge + HALO), :] = correct(rim_ref[pl.ds(0, edge + HALO), lanes], dead)
        c_ref[pl.ds(span, edge + HALO), :] = correct(rim_ref[pl.ds(edge + HALO, edge + HALO), lanes], dead)
        c_ref[pl.ds(span + edge + HALO, HALO), :] = correct(jnp.where(even, near, far), dead) * has_down
        for half in range(2):
            for r in range(edge // tile):
                acc = band_sum(c_ref, half * span + HALO + r * tile, tile, width)
                first = begin + half * (rows - edge) + r * tile
                t = first + lax.broadcasted_iota(jnp.int32, (tile, LANE), 0)
                terms = jnp.minimum(t + width, nframes - 1) - jnp.maximum(t - width, 0) + 1
                smoothed = (acc / terms.astype(f32)).astype(bf16)
                out_ref[pl.ds(half * edge + r * tile, tile), lanes] = smoothed
                (top_ref, bottom_ref)[half][pl.ds(r * tile, tile), lanes] = smoothed


def smooth_middle(frames, dead, width, edge):
    rows, px = frames.shape
    mid = rows - 2 * edge
    return kernel_call(
        middle_kernel,
        "smooth_middle",
        (frames, dead, width),
        [((mid, px), bf16), ((2 * (edge + HALO), px), bf16)],
        [pltpu.VMEM((mid + 2 * HALO, LANE), f32)],
    )


def smooth_edges(rim, near, far, dead, width, nframes):
    edge = rim.shape[0] // 2 - HALO
    return kernel_call(
        functools.partial(edge_kernel, nframes=nframes),
        "smooth_edges",
        (rim, near, far, dead, width),
        [((2 * edge, rim.shape[1]), bf16)] + [((edge, rim.shape[1]), bf16)] * 2,
        [pltpu.VMEM((2 * (edge + 2 * HALO), LANE), f32)],
    )


def hold_kernel(*refs):
    pass


def hold(x, *tokens):
    anywhere = pl.BlockSpec(memory_space=pl.ANY)
    return pl.pallas_call(
        hold_kernel,
        in_specs=[anywhere] * (1 + len(tokens)),
        out_specs=anywhere,
        out_shape=jax.ShapeDtypeStruct(x.shape, x.dtype),
        input_output_aliases={0: 0},
        compiler_params=pltpu.CompilerParams(vmem_limit_bytes=2**20),
        cost_estimate=pl.CostEstimate(flops=0, bytes_accessed=0, transcendentals=0),
        name="hold",
    )(x, *tokens)


def tree_order(bits):
    return [(high << bits[0]) + slot for high in range(2) for slot in tree_order(bits[1:])] if bits else [0]


def centre(product_ref, total_ref, mean, keep_ref, send_ref, bits):
    rows = product_ref.shape[0] // CYCLES - 16
    half = 2 ** len(bits) // 2
    size = rows // (2 * half)
    me = lax.axis_index("pixel")
    for at, slot in enumerate(tree_order(bits)):
        out_ref = send_ref if at >= half else keep_ref
        place = (at % half) * CYCLES * size
        for q in range(CYCLES):
            begin = pl.multiple_of(q * rows + (me ^ slot) * size, size)
            total = total_ref[pl.ds(begin, size), :]
            for j in range(keep_ref.shape[1] // LANE):
                lanes = pl.ds(j * LANE, LANE)
                centred = product_ref[pl.ds(begin, size), lanes] - total * mean[q][:, j * LANE : (j + 1) * LANE]
                out_ref[pl.ds(place + q * size, size), lanes] = centred.astype(bf16)


def means(product_ref, total_ref, width):
    base = product_ref.shape[0] - 16 * CYCLES
    count = [total_ref[pl.ds(base + 16 * q, 1), :][:, :1] for q in range(CYCLES)]
    mean = [product_ref[pl.ds(base + 16 * q, 1), pl.ds(0, width)] / jnp.maximum(count[q], 1.0) for q in range(CYCLES)]
    return mean, count


def split(x, pieces):
    out = []
    for _ in range(pieces):
        out.append(x.astype(bf16).astype(f32))
        x = x - out[-1]
    return out


def stat_rows(mean, count=None):
    width = mean[0].shape[1]
    rows = [piece for m in zip(*[split(m, 2 if count is None else 3) for m in mean]) for piece in m]
    zero = jnp.zeros((1, width), f32)
    if count is not None:
        lane = lax.broadcasted_iota(jnp.int32, (1, width), 1) // (LANE // 2)
        for part in zip(*[split(c, 2) for c in count]):
            rows.append(sum(jnp.where(lane == q, p, 0.0) for q, p in enumerate(part)))
    return jnp.concatenate(rows + [zero] * (STAT_ROWS - len(rows)), axis=0).astype(bf16)


def gram_own_kernel(label_ref, valid_ref, mid_ref, edge_ref, *refs, groups):
    near_refs, (out_ref, left_ref, total_ref, acc_ref) = refs[:-4], refs[-4:]
    px = mid_ref.shape[1]
    rim = edge_ref.shape[0] // 2
    rows = mid_ref.shape[0] + 2 * rim
    width = 2 * rows
    label = label_ref[...][None, :]
    used = valid_ref[...][None, :] == 1
    for q in range(CYCLES):
        weight = jnp.broadcast_to(((label == q) & used).astype(f32), (16, px)).astype(bf16)
        left_ref[pl.ds(q * rows, rim), :] = edge_ref[pl.ds(0, rim), :] * weight[:1]
        left_ref[pl.ds(q * rows + rim, rows - 2 * rim), :] = mid_ref[...] * weight[:1]
        left_ref[pl.ds((q + 1) * rows - rim, rim), :] = edge_ref[pl.ds(rim, rim), :] * weight[:1]
        left_ref[pl.ds(CYCLES * rows + 16 * q, 16), :] = weight
    right = jnp.concatenate([ref[...] for ref in (mid_ref, edge_ref, *near_refs)] + [jnp.ones((LANE, px), bf16)], axis=0)
    acc_ref[...] = lax.dot_general(left_ref[...], right, NT, preferred_element_type=f32)
    total_ref[...] = acc_ref[:, pl.ds(width, LANE)]
    mean, count = means(acc_ref, total_ref, width)
    size = rows // groups
    stats = stat_rows(mean, count)
    for group in range(groups):
        for q in range(CYCLES):
            here = pl.ds(q * rows + group * size, size)
            for j in range(width // LANE):
                lanes = pl.ds(j * LANE, LANE)
                centred = acc_ref[here, lanes] - total_ref[here, :] * mean[q][:, j * LANE : (j + 1) * LANE]
                out_ref[group, pl.ds(q * size, size), lanes] = centred.astype(bf16)
        out_ref[group, pl.ds(CYCLES * size, STAT_ROWS), :] = stats


def part_outs(rows, width, stat_rows):
    return [((rows, width), bf16), ((rows + stat_rows, width), bf16), ((stat_rows, width), bf16)]


def gram_own(label, valid, mid, edge, near, groups):
    px = mid.shape[1]
    rows = mid.shape[0] + edge.shape[0]
    tall = CYCLES * (rows + 16)
    return kernel_call(
        functools.partial(gram_own_kernel, groups=groups),
        "gram_own",
        (label, valid, mid, edge, *near),
        [((groups, CYCLES * rows // groups + STAT_ROWS, 2 * rows), bf16), ((tall, px), bf16), ((tall, LANE), f32)],
        [pltpu.VMEM((tall, 2 * rows + LANE), f32)],
        mib=10,
    )


def gram_cross_kernel(left_ref, total_ref, *refs, bits, cols, at):
    keep_ref, send_ref, stat_ref, acc_ref = refs[-4:]
    right = jnp.concatenate([ref[...] for ref in refs[:cols]], axis=0)
    acc_ref[...] = lax.dot_general(left_ref[...], right, NT, preferred_element_type=f32)
    mean, _ = means(acc_ref, total_ref, acc_ref.shape[1])
    here = pl.ds(at, acc_ref.shape[1])
    stats = stat_rows(mean)
    stat_ref[:, here] = stats
    send_ref[pl.ds(send_ref.shape[0] - STAT_ROWS, STAT_ROWS), here] = stats
    centre(acc_ref, total_ref, mean, keep_ref.at[:, here], send_ref.at[:, here], bits)


def gram_cross(left, total, cols, width, at, part, bits):
    tall = left.shape[0]
    return kernel_call(
        functools.partial(gram_cross_kernel, bits=bits, cols=len(cols), at=at),
        "gram_cross",
        (left, total, *cols, *part),
        part_outs(tall // 2 - 16, width, STAT_ROWS),
        [pltpu.VMEM((tall, sum(c.shape[0] for c in cols)), f32)],
        mib=10,
        aliases={2 + len(cols) + i: i for i in range(len(part))},
    )


def join_stats(mine_ref, got_ref, groups):
    mine = mine_ref[...].astype(f32)
    got = got_ref[pl.ds(got_ref.shape[0] - mine.shape[0], mine.shape[0]), :].astype(f32)
    return jnp.concatenate([mine[: groups * SENT], got[: groups * SENT]], axis=0)


def merge_kernel(keep_ref, got_ref, stat_ref, next_keep_ref, next_send_ref, next_stat_ref, *, groups):
    half = next_keep_ref.shape[0]
    total = keep_ref[...].astype(f32) + got_ref[pl.ds(0, 2 * half), :].astype(f32)
    next_keep_ref[...] = total[:half].astype(bf16)
    next_send_ref[pl.ds(0, half), :] = total[half:].astype(bf16)
    stats = join_stats(stat_ref, got_ref, groups).astype(bf16)
    next_stat_ref[...] = stats
    next_send_ref[pl.ds(half, stats.shape[0]), :] = stats


def merge(keep, got, stat, groups):
    outs = part_outs(keep.shape[0] // 2, keep.shape[1], 2 * groups * SENT)
    return kernel_call(functools.partial(merge_kernel, groups=groups), "merge", (keep, got, stat), outs)


def whole_means(stats):
    n = stats.shape[0]
    return stats + pltpu.roll(stats, n - CYCLES, 0) + pltpu.roll(stats, n - 2 * CYCLES, 0)


def own_part_kernel(got_ref, out_ref, side_ref, share_ref, *, edge):
    groups, _, width = got_ref.shape
    size = out_ref.shape[0] // CYCLES
    rows = width // 2
    mid = rows - 2 * edge
    me = lax.axis_index("pixel")
    stats = [got_ref[me ^ i, pl.ds(CYCLES * size, STAT), :].astype(f32) for i in range(groups)]
    stats = jnp.concatenate(stats, axis=0)
    entries = stats.shape[0]
    kind = lax.broadcasted_iota(jnp.int32, (entries, 1), 0) % STAT
    n = me * size + lax.broadcasted_iota(jnp.int32, (size, rows), 0)
    packed = jnp.where(n < edge, n + mid, jnp.where(n < edge + mid, n - edge, n))
    pick = (packed == lax.broadcasted_iota(jnp.int32, (size, rows), 1)).astype(f32)
    counted = stats + pltpu.roll(stats, entries - 1, 0)
    mean = whole_means(stats)
    for q in range(CYCLES):
        number = pltpu.roll(counted, entries - 3 * CYCLES + q, 0)[:, q * LANE // 2 : q * LANE // 2 + 1]
        number = jnp.where(kind == q, number, 0.0)
        count = jnp.sum(number, axis=0, keepdims=True)
        share = number / count
        share_ref[pl.ds(q * entries, entries), :] = jnp.broadcast_to(share, (entries, LANE))
        share_ref[pl.ds(CYCLES * entries + 8 * q, 8), :] = jnp.broadcast_to(1.0 / count, (8, LANE))
        apart = mean[:, :rows] - jnp.sum(mean[:, :rows] * share, axis=0, keepdims=True)
        side = lax.dot_general(pick, apart * share, NT, precision=EXACT, preferred_element_type=f32)
        here = pl.ds(q * size, size)
        side_ref[here, :] = side
        within = got_ref[0, here, :].astype(f32)
        for group in range(1, groups):
            within += got_ref[group, here, :].astype(f32)
        out_ref[here, :] = within * (1.0 / count) + part_between(mean, side, share)


def part_between(mean, side, share):
    apart = mean - jnp.sum(mean * share, axis=0, keepdims=True)
    return lax.dot_general(side, apart, NN, precision=EXACT, preferred_element_type=f32)


def part_sum(keep_ref, got_ref, mean, side, share, inverse, q):
    size = keep_ref.shape[0] // CYCLES
    rows = pl.ds(q * size, size)
    within = keep_ref[rows, :].astype(f32) + got_ref[rows, :].astype(f32)
    return within * inverse + part_between(mean, side, share)


def part_sums(keep_ref, got_ref, stat_ref, side_ref, share_ref, bits):
    stats = join_stats(stat_ref, got_ref, 2 ** len(bits) // 2)
    spots = [sum((group >> bit & 1) << level for level, bit in enumerate(bits)) for group in range(2 ** len(bits))]
    stats = stats + pltpu.roll(stats, stats.shape[0] - CYCLES, 0)
    zero = jnp.zeros((STAT - SENT, stats.shape[1]), f32)
    stats = jnp.concatenate([x for spot in spots for x in (stats[SENT * spot : SENT * (spot + 1)], zero)], axis=0)
    entries = stats.shape[0]
    mean = stats
    size = keep_ref.shape[0] // CYCLES
    return [
        part_sum(
            keep_ref,
            got_ref,
            mean,
            side_ref[pl.ds(q * size, size), :],
            share_ref[pl.ds(q * entries, entries), :][:, :1],
            share_ref[pl.ds(CYCLES * entries + 8 * q, 1), :][:, :1],
            q,
        )
        for q in range(CYCLES)
    ]


def own_part(got, edge):
    groups, tall, width = got.shape
    size = (tall - STAT_ROWS) // CYCLES
    entries = groups * STAT
    outs = [((CYCLES * size, width), f32), ((CYCLES * size, entries), f32), ((CYCLES * (entries + 8), LANE), f32)]
    return kernel_call(functools.partial(own_part_kernel, edge=edge), "own_part", (got,), outs)


def finish_kernel(own_ref, side_ref, share_ref, *refs, parts, rows, edge, orders):
    refs, out_ref = refs[:-1], refs[-1]
    size = out_ref.shape[0]
    mid = rows - 2 * edge
    me = lax.axis_index("frame")
    sums = [[ref[pl.ds(q * size, size), :] for q in range(CYCLES)] for ref in (own_ref,)]
    sums += [part_sums(*refs[i : i + 3], side_ref, share_ref, orders[i // 3 % 2]) for i in range(0, len(refs), 3)]
    for q in range(CYCLES):
        for j, places in enumerate(parts):
            pieces = [sums[part][q][:, at : at + n] for (part, at), n in zip(places, (mid, edge, edge))]
            natural = jnp.concatenate([pieces[1], pieces[0], pieces[2]], axis=1)
            out_ref[:, q, pl.ds(pl.multiple_of((me ^ j) * rows, rows), rows)] = natural


def swap(x, axis, bit):
    return lax.ppermute(x, axis, [(i, i ^ bit) for i in range(lax.axis_size(axis))])


def swap_pieces(x, *cuts):
    at = [0] + [x.shape[0] * cut // 16 for cut in cuts] + [x.shape[0]]
    return [swap(x[i:j], "frame", 1) for i, j in zip(at, at[1:])]


def shards(frames, dead_time, band_width, cycle_label, valid):
    nblocks = lax.axis_size("frame")
    ngroups = lax.axis_size("pixel")
    rows = frames.shape[0]
    nframes = rows * nblocks
    own_rows = rows // ngroups
    edge_rows = max(rows // EDGE_PART, 32)
    mid_rows = rows - 2 * edge_rows
    chip = lax.axis_index("frame") // 2
    even = lax.axis_index("frame") % 2 == 0

    near_halo, far_halo = halos(frames)
    mid, rim = smooth_middle(frames, dead_time, band_width, edge_rows)
    halo = far_halo
    for bit in sorted({x ^ (x + 1) for x in range(nblocks // 2 - 1)}):
        got = swap(far_halo, "frame", 2 * bit)
        wanted = (chip ^ bit) == jnp.where(even, chip + 1, chip - 1)
        halo = got if bit == 1 else jnp.where(wanted, got, halo)
    mid = hold(mid, halo)
    far_mid = {j: swap(mid, "frame", j) for j in range(2, nblocks, 2)}
    near_halo = swap(near_halo, "frame", 1)
    halo = swap(hold(halo, mid), "frame", 1)
    near = swap_pieces(mid, 8)
    edge, top, bottom = smooth_edges(rim, near_halo, halo, dead_time, band_width, nframes)
    far_ends = {j: [swap(x, "frame", j) for x in (top, bottom)] for j in range(2, nblocks, 2)}
    near += swap_pieces(edge, 8)

    levels = ngroups.bit_length() - 1
    straight = tuple(range(levels))
    orders = [straight, (straight[:2][::-1] + straight[2:])]
    own, left, total = gram_own(cycle_label, valid, mid, edge, near, ngroups)
    wait = [total]
    own, side, share = own_part(lax.all_to_all(own, "pixel", 0, 0, tiled=True), edge_rows)

    sizes = (mid_rows, edge_rows, edge_rows)
    split = [[(0,)], [(1,), (2,)] if 2 * edge_rows % LANE == 0 else [(1, 2)]]
    others = []
    parts = [[(0, i * rows), (0, i * rows + mid_rows), (0, i * rows + mid_rows + edge_rows)] for i in range(2)]
    for j in range(2, nblocks, 2):
        places = [[None] * 3, [None] * 3]
        pieces = [far_mid[j], *far_ends[j]]
        for part in split:
            width = 2 * sum(sizes[k] for group in part for k in group)
            at, done = 0, ()
            bits = orders[len(others) // 3 % 2]
            for group in part:
                group_rows = sum(sizes[k] for k in group)
                far, near = [], []
                for k in group:
                    for i in range(2):
                        places[i][k] = (1 + len(others) // 3, at + i * group_rows + sum(x.shape[0] for x in far))
                    far.append(hold(pieces[k], *wait))
                    near += swap_pieces(far[-1], *FORWARDS[k])
                done = gram_cross(left, total, far + near, width, at, done, bits)
                at += 2 * group_rows
                wait = [done[2]]
            keep, send, stat = done
            for level in range(levels):
                got = swap(send, "pixel", 1 << bits[level])
                if level + 1 < levels:
                    keep, send, stat = merge(keep, got, stat, 2**level)
            others += [keep, got, stat]
        parts += places
    return kernel_call(
        functools.partial(finish_kernel, parts=parts, rows=rows, edge=edge_rows, orders=orders),
        "finish",
        (own, side, share, *others),
        [((own_rows, CYCLES, nframes), f32)],
    )[0]


def solution(mesh):
    in_specs = (P("frame", "pixel"), P("pixel"), P("pixel"), P("pixel"), P("pixel"))
    out_specs = P(("frame", "pixel"), None, None)
    return jax.shard_map(shards, mesh=mesh, in_specs=in_specs, out_specs=out_specs, check_vma=False)
```
